256 devices in a mesh: prompt: 8 (over x, core), grp: 32 (over y, z).
Axes of the slice: x: 4, y: 4, z: 8, core: 2. Of those that a mesh axis runs over, the one named last changes fastest.
Arguments:
- queries: bfloat16 [256, 256, 1024], P(('prompt', 'grp')), parts along dimension 0, may hold values from -130 to 130
- resp_keys: bfloat16 [256, 256, 128], P(('prompt', 'grp')), parts along dimension 0, may hold values from -6 to 6
- resp_values: bfloat16 [256, 256, 128], P(('prompt', 'grp')), parts along dimension 0, may hold values from -6 to 6
- prefix_keys: bfloat16 [16384, 128], P(('prompt', 'grp')), parts along dimension 0, may hold values from -6 to 6
- prefix_values: bfloat16 [16384, 128], P(('prompt', 'grp')), parts along dimension 0, may hold values from -6 to 6
- out_grad: bfloat16 [256, 256, 1024], P(('prompt', 'grp')), parts along dimension 0, may hold values from -6 to 6
- lengths: int32 [256], P('prompt'), parts along dimension 0, may hold values from 1 to 256, 4096 in all
- loss_mask: int32 [256, 256], P(('prompt', 'grp')), parts along dimension 0, may hold values 0 or 1
Outputs:
- attended: bfloat16 [256, 256, 1024], P(('prompt', 'grp')), parts along dimension 0
- query_grad: bfloat16 [256, 256, 1024], P(('prompt', 'grp')), parts along dimension 0
- resp_key_grad: bfloat16 [256, 256, 128], P(('prompt', 'grp')), parts along dimension 0
- resp_value_grad: bfloat16 [256, 256, 128], P(('prompt', 'grp')), parts along dimension 0
- prefix_key_grad: bfloat16 [16384, 128], P(('prompt', 'grp')), parts along dimension 0
- prefix_value_grad: bfloat16 [16384, 128], P(('prompt', 'grp')), parts along dimension 0
The draws below stay inside these ranges and needn't reach their ends.
There are 8 independent parts, one for each index of `prompt`. The reference program is written for one: setup_inputs(seed, part) draws one part's arguments, and reference() takes and returns one part's arrays. A program takes and returns all parts, laid end to end along the dimension named above; each array names one. Nothing has to cross between parts.
Inputs may be any that keep to these rules, and one draw needn't show every extreme that they name: The lengths of a prompt's 32 responses sum to 4096 and the longest is exactly 256.
All inputs are finite; a program needn't handle non-finite values. No bound on the sum of `loss_mask` on one device may be relied on, other than what follows from the above.
Results may differ from the reference program's by a relative error of at most 0.038.
Values may be sent and summed in bfloat16 or wider, within the bound.
No kernel may reach another device: no remote copies, remote signals or barrier semaphores. Data moves between devices by JAX's collectives and lax.ppermute only.
A program may use at most 64 MiB of HBM per device.

```python
import math
import jax
import jax.numpy as jnp
import numpy as np
from jax import lax

HEADS = 8
HEAD_DIM = 128
RESP = 256
RESPONSES = 32
PREFIX = 2048


def draw_queries(key, part):
    key = jax.random.fold_in(key, 21)
    drawn = 2.5 * jnp.clip(jax.random.normal(key, (RESPONSES, RESP, HEADS, HEAD_DIM), jnp.float32), -6.0, 6.0)
    return drawn.reshape(RESPONSES, RESP, HEADS * HEAD_DIM).astype(jnp.bfloat16)


def draw_prefix_keys(key, part):
    key = jax.random.fold_in(key, 22)
    drawn = jnp.clip(jax.random.normal(key, (PREFIX, HEAD_DIM), jnp.float32), -6.0, 6.0)
    return drawn.astype(jnp.bfloat16)


def touch_ends(entries, key, least, top_value):
    longest = entries.shape.index(max(entries.shape))
    spots = []
    for shift in (0, 1):
        where = [jax.random.randint(jax.random.fold_in(key, axis), (), 0, length) for axis, length in enumerate(entries.shape)]
        where[longest] = (where[longest] + shift) % entries.shape[longest]
        spots.append(tuple(where))
    return entries.at[spots[0]].set(least).at[spots[1]].set(top_value)


def block_scale(key, shape, shards, low, high):
    def one(axis_at, parts):
        draws = jax.random.uniform(jax.random.fold_in(jax.random.fold_in(key, 6), axis_at), (parts,), jnp.float32, low / len(shards), high / len(shards))
        return jnp.repeat(jnp.exp(draws), shape[axis_at] // parts).reshape((-1,) + (1,) * (len(shape) - axis_at - 1))

    loudness = one(*shards[0])
    for cut in shards[1:]:
        loudness = loudness * one(*cut)
    return loudness


def profile(amount, total, bound, lean):
    portions = [(1 << 20) // math.isqrt(grade ** lean) + 1 for grade in range(2, amount + 1)]
    spare, given = total - bound - (amount - 1), [1] * (amount - 1)
    while spare > 0:
        candidates = [i for i in range(amount - 1) if given[i] < bound]
        mass, left = sum([portions[i] for i in candidates]), spare
        for i in candidates:
            extra = min(bound - given[i], max(1, left * portions[i] // mass), spare)
            given[i] = given[i] + extra
            spare = spare - extra
    return np.array([bound] + given)


def ragged(rng, amount, total, bound, lean):
    if amount == 2:
        one = jax.random.randint(rng, (), max(1, total - bound), min(bound, total - 1) + 1)
        return jnp.stack([one, total - one])
    sizes = jnp.asarray(profile(amount, total, bound, lean), jnp.int32)
    twos = (amount - 1) // 2
    donor, taker = sizes[1:1 + 2 * twos:2], sizes[2:2 + 2 * twos:2]
    margin = jnp.minimum(donor - 1, bound - taker)
    shifted = jax.random.randint(jax.random.fold_in(rng, 1), (twos,), 0, 1 << 20) % (margin + 1)
    sizes = sizes.at[1:1 + 2 * twos:2].set(donor - shifted).at[2:2 + 2 * twos:2].set(taker + shifted)
    return sizes[jax.random.permutation(jax.random.fold_in(rng, 2), amount)]


def scatter_about(key, dims, width, reach, shards=(), kind=jnp.bfloat16):
    values = width * jax.random.normal(key, dims, jnp.float32)
    if shards:
        values = values * block_scale(key, dims, shards, -0.22, 0.18)
    return jnp.clip(values, -reach, reach).astype(kind)


def setup_inputs(seed: int = 0, part: int = 0) -> dict:
    seeds = jax.random.split(jax.random.key(seed), 9)
    part_keys = jax.random.split(jax.random.fold_in(seeds[8], part), 9)
    return {
        "queries": draw_queries(jax.random.fold_in(jax.random.fold_in(seeds[8], part), 71), part),
        "resp_keys": scatter_about(part_keys[1], (RESPONSES, RESP, HEAD_DIM), 1.0, 6.0, ((0, 32),)),
        "resp_values": scatter_about(part_keys[2], (RESPONSES, RESP, HEAD_DIM), 1.0, 6.0, ((0, 32),)),
        "prefix_keys": draw_prefix_keys(jax.random.fold_in(jax.random.fold_in(seeds[8], part), 71), part),
        "prefix_values": scatter_about(part_keys[4], (PREFIX, HEAD_DIM), 1.0, 6.0, ((0, 32),)),
        "out_grad": scatter_about(part_keys[5], (RESPONSES, RESP, HEADS * HEAD_DIM), 1.0, 6.0, ((0, 32),)),
        "lengths": ragged(part_keys[6], RESPONSES, RESP * RESPONSES // 2, RESP, 2).astype(jnp.int32),
        "loss_mask": touch_ends((jax.random.randint(part_keys[7], (RESPONSES, RESP), 0, 8) < 7).astype(jnp.int32), jax.random.fold_in(part_keys[7], 1), 0, 1),
    }


neg_big = -1e30


def partial_sums(scores, values):
    maximum = jnp.max(scores, axis=1)
    weights = jnp.exp(scores - maximum[:, None])
    totals = jnp.sum(weights, axis=1)
    summed = jnp.dot(weights.astype(jnp.bfloat16), values, preferred_element_type=jnp.float32)
    return maximum, totals, summed


def grad_terms(scores, row_block, grad_rows, log_total, inner_dot, key_rows, values, softmax_scale):
    probability = jnp.exp(scores - log_total[:, None])
    prob_grad = jnp.dot(grad_rows, values.T, preferred_element_type=jnp.float32)
    dscore = (probability * (prob_grad - inner_dot[:, None])).astype(jnp.bfloat16)
    dquery = jnp.dot(dscore, key_rows, preferred_element_type=jnp.float32) * softmax_scale
    key_grad = jnp.dot(dscore.T, row_block, preferred_element_type=jnp.float32) * softmax_scale
    dvalue = jnp.dot(probability.astype(jnp.bfloat16).T, grad_rows, preferred_element_type=jnp.float32)
    return dquery, key_grad, dvalue


def response_pass(query_block, key_block, value_block, grad_block, keep_block, length_value, prefix_keys, prefix_values):
    softmax_scale = HEAD_DIM ** -0.5
    row_block = query_block.reshape(RESP * HEADS, HEAD_DIM)
    row_pos = jnp.arange(RESP * HEADS) // HEADS
    alive = row_pos < length_value
    key_pos = jnp.arange(RESP)
    allowed = (key_pos[None, :] <= row_pos[:, None]) & (key_pos[None, :] < length_value)
    pre_scores = jnp.dot(row_block, prefix_keys.T, preferred_element_type=jnp.float32) * softmax_scale
    own_scores = jnp.where(allowed, jnp.dot(row_block, key_block.T, preferred_element_type=jnp.float32) * softmax_scale, neg_big)
    pre_max, pre_total, pre_sum = partial_sums(pre_scores, prefix_values)
    own_max, own_total, own_sum = partial_sums(own_scores, value_block)
    maximum = jnp.maximum(pre_max, own_max)
    pre_weight = jnp.exp(pre_max - maximum)
    own_weight = jnp.exp(own_max - maximum)
    totals = pre_weight * pre_total + own_weight * own_total
    blended = (pre_weight[:, None] * pre_sum + own_weight[:, None] * own_sum) / totals[:, None]
    attended = jnp.where(alive[:, None], blended, 0.0).astype(jnp.bfloat16)
    log_total = maximum + jnp.log(totals)
    kept = alive & (jnp.repeat(keep_block, HEADS) == 1)
    grad_rows = jnp.where(kept[:, None], grad_block.reshape(RESP * HEADS, HEAD_DIM), jnp.zeros((), jnp.bfloat16))
    inner_dot = jnp.sum(grad_rows.astype(jnp.float32) * attended.astype(jnp.float32), axis=1)
    pre_query, pre_key, pre_value = grad_terms(pre_scores, row_block, grad_rows, log_total, inner_dot, prefix_keys, prefix_values, softmax_scale)
    own_query, own_key, own_value = grad_terms(own_scores, row_block, grad_rows, log_total, inner_dot, key_block, value_block, softmax_scale)
    query_grad = (pre_query + own_query).astype(jnp.bfloat16)
    return (attended.reshape(RESP, HEADS * HEAD_DIM), query_grad.reshape(RESP, HEADS * HEAD_DIM), own_key.astype(jnp.bfloat16), own_value.astype(jnp.bfloat16), pre_key, pre_value)


def reference(queries, resp_keys, resp_values, prefix_keys, prefix_values, out_grad, lengths, loss_mask):
    def one_response(carried, items):
        results = response_pass(items[0], items[1], items[2], items[3], items[4], items[5], prefix_keys, prefix_values)
        return (carried[0] + results[4], carried[1] + results[5]), (results[0], results[1], results[2], results[3])

    zeros_grad = jnp.zeros((PREFIX, HEAD_DIM), jnp.float32)
    sums_out, stacked = lax.scan(one_response, (zeros_grad, zeros_grad), (queries, resp_keys, resp_values, out_grad, loss_mask, lengths))
    return (stacked[0], stacked[1], stacked[2], stacked[3], sums_out[0].astype(jnp.bfloat16), sums_out[1].astype(jnp.bfloat16))
```

```python
import math
import jax, jax.numpy as jnp
from jax import lax
from jax.experimental import pallas as pl
from jax.experimental.pallas import tpu as pltpu
from jax.sharding import PartitionSpec as P
NEG=-1e30
KT=256
def NN(a,b): return jnp.dot(a,b,preferred_element_type=jnp.float32)
def NTd(a,b): return lax.dot_general(a,b,(((1,),(1,)),((),())),preferred_element_type=jnp.float32)
def body(len_ref, q_ref, do_ref, mask_ref, kr_ref, vr_ref, kv_ref,
         att_ref, dq_ref, dkr_ref, dvr_ref, dkv_ref,
         kt_s, vt_s, s_s, w_s, dk_s, dv_s):
    h=pl.program_id(0); nh=pl.num_programs(0)
    D=128; T=256; PN=kv_ref.shape[0]; nt=PN//KT
    scale=D**-0.5; c=scale*math.log2(math.e)
    L=len_ref[0]
    def ktile(i): return kr_ref[...] if i==nt else kv_ref[i*KT:(i+1)*KT,0:D]
    def vtile(i): return vr_ref[...] if i==nt else kv_ref[i*KT:(i+1)*KT,D:2*D]
    @pl.when(h==0)
    def _():
        for i in range(nt+1):
            kt_s[:,i*KT:(i+1)*KT]=ktile(i).T
            vt_s[:,i*KT:(i+1)*KT]=vtile(i).T
        dk_s[...]=jnp.zeros_like(dk_s); dv_s[...]=jnp.zeros_like(dv_s)
    q=q_ref[...]
    qT=q.T
    tpos=lax.broadcasted_iota(jnp.int32,(1,T),1)
    alive=tpos<L
    keep=alive&(mask_ref[...]==1)
    mx=jnp.full((8,T),-jnp.inf,jnp.float32)
    for i in [nt]+list(range(nt)):
        s=NN(ktile(i),qT)
        if i==nt:
            u=lax.broadcasted_iota(jnp.int32,(KT,T),0); t=lax.broadcasted_iota(jnp.int32,(KT,T),1)
            s=jnp.where((u<=t)&(u<L),s,NEG)
        s_s[i*KT:(i+1)*KT,:]=s
        mx=jnp.maximum(mx,jnp.max(s.reshape(KT//8,8,T),axis=0))
    m=jnp.max(mx,axis=0,keepdims=True)
    l8=jnp.zeros((8,T),jnp.float32)
    oT=jnp.zeros((D,T),jnp.float32)
    for i in [nt]+list(range(nt)):
        w=jnp.exp2((s_s[i*KT:(i+1)*KT,:]-m)*c)
        l8=l8+jnp.sum(w.reshape(KT//8,8,T),axis=0)
        wb=w.astype(jnp.bfloat16)
        w_s[i*KT:(i+1)*KT,:]=wb
        oT=oT+NN(vt_s[:,i*KT:(i+1)*KT],wb)
    rcp=1.0/jnp.sum(l8,axis=0,keepdims=True)
    attT=jnp.where(alive,oT*rcp,0.0).astype(jnp.bfloat16)
    att_ref[...]=attT.T
    gT=jnp.where(keep,do_ref[...].T.astype(jnp.float32)*rcp,0.0)
    gTb=gT.astype(jnp.bfloat16)
    inner=jnp.sum(gTb.astype(jnp.float32)*attT.astype(jnp.float32),axis=0,keepdims=True)
    g=gTb.T
    dqT=jnp.zeros((D,T),jnp.float32)
    for i in [nt]+list(range(nt)):
        sl=slice(i*KT,(i+1)*KT)
        pg=NN(vtile(i),gTb)
        wb=w_s[sl,:]
        ds=(wb.astype(jnp.float32)*(pg-inner)).astype(jnp.bfloat16)
        dqT=dqT+NN(kt_s[:,sl],ds)
        dk_s[sl,:]+=NN(ds,q)
        dv_s[sl,:]+=NN(wb,g)
    dq_ref[...]=(dqT*scale).astype(jnp.bfloat16).T
    @pl.when(h==nh-1)
    def _():
        dkv_ref[:,0:D]=(dk_s[0:PN,:]*scale).astype(jnp.bfloat16)
        dkv_ref[:,D:2*D]=dv_s[0:PN,:].astype(jnp.bfloat16)
        dkr_ref[...]=(dk_s[PN:,:]*scale).astype(jnp.bfloat16)
        dvr_ref[...]=dv_s[PN:,:].astype(jnp.bfloat16)
def attn(length,q,do,mask,kr,vr,kv):
    T,F=q.shape; D=kr.shape[1]; H=F//D; PN=kv.shape[0]; N=PN+T
    full=lambda s: pl.BlockSpec(s,lambda h:(0,)*len(s))
    return pl.pallas_call(body,grid=(H,),
        in_specs=[pl.BlockSpec(memory_space=pltpu.SMEM),pl.BlockSpec((T,D),lambda h:(0,h)),pl.BlockSpec((T,D),lambda h:(0,h)),
                  full((1,T)),full((T,D)),full((T,D)),full((PN,2*D))],
        out_specs=[pl.BlockSpec((T,D),lambda h:(0,h)),pl.BlockSpec((T,D),lambda h:(0,h)),full((T,D)),full((T,D)),full((PN,2*D))],
        out_shape=[jax.ShapeDtypeStruct((T,F),jnp.bfloat16),jax.ShapeDtypeStruct((T,F),jnp.bfloat16),jax.ShapeDtypeStruct((T,D),jnp.bfloat16),jax.ShapeDtypeStruct((T,D),jnp.bfloat16),jax.ShapeDtypeStruct((PN,2*D),jnp.bfloat16)],
        scratch_shapes=[pltpu.VMEM((D,N),jnp.bfloat16),pltpu.VMEM((D,N),jnp.bfloat16),pltpu.VMEM((N,T),jnp.float32),pltpu.VMEM((N,T),jnp.bfloat16),pltpu.VMEM((N,D),jnp.float32),pltpu.VMEM((N,D),jnp.float32)],
        compiler_params=pltpu.CompilerParams(vmem_limit_bytes=50*2**20),
        name="attn")(length,q,do,mask,kr,vr,kv)


Z_SIZE = 8


def shards(queries, resp_keys, resp_values, prefix_keys, prefix_values, out_grad, lengths, loss_mask):
    group_count = lax.axis_size("grp")
    z_size = Z_SIZE
    y_size = group_count // z_size
    z_groups = [[y * z_size + z for z in range(z_size)] for y in range(y_size)]
    y_groups = [[y * z_size + z for y in range(y_size)] for z in range(z_size)]
    my_index = lax.axis_index("grp")
    length_here = lax.dynamic_slice_in_dim(lengths, my_index, 1, 0)
    block = jnp.concatenate([prefix_keys, prefix_values], axis=1)
    rows, width = block.shape
    plane = lax.all_to_all(
        jnp.broadcast_to(block[None], (z_size, rows, width)), "grp", 0, 0, axis_index_groups=z_groups, tiled=True
    ).reshape(z_size * rows, width)
    whole = lax.all_to_all(
        jnp.broadcast_to(plane[None], (y_size, z_size * rows, width)), "grp", 0, 0, axis_index_groups=y_groups, tiled=True
    ).reshape(group_count * rows, width)
    attended, query_grad, key_grad, value_grad, terms = attn(
        length_here, queries[0], out_grad[0], loss_mask, resp_keys[0], resp_values[0], whole
    )
    part = lax.all_to_all(
        terms.reshape(y_size, z_size * rows, width), "grp", 0, 0, axis_index_groups=y_groups, tiled=True
    )
    part = jnp.sum(part.astype(jnp.float32), axis=0).astype(jnp.bfloat16)
    part = lax.all_to_all(
        part.reshape(z_size, rows, width), "grp", 0, 0, axis_index_groups=z_groups, tiled=True
    )
    share = jnp.sum(part.astype(jnp.float32), axis=0).astype(jnp.bfloat16)
    head = width // 2
    return (attended[None], query_grad[None], key_grad[None], value_grad[None], share[:, :head], share[:, head:])


def solution(mesh):
    placed = (
        P(("prompt", "grp"), None, None),
        P(("prompt", "grp"), None, None),
        P(("prompt", "grp"), None, None),
        P(("prompt", "grp"), None),
        P(("prompt", "grp"), None),
        P(("prompt", "grp"), None, None),
        P("prompt"),
        P(("prompt", "grp"), None),
    )
    return jax.shard_map(
        shards,
        mesh=mesh,
        in_specs=placed,
        out_specs=(
            P(("prompt", "grp"), None, None),
            P(("prompt", "grp"), None, None),
            P(("prompt", "grp"), None, None),
            P(("prompt", "grp"), None, None),
            P(("prompt", "grp"), None),
            P(("prompt", "grp"), None),
        ),
        check_vma=False,
    )
```

```python
import math
import jax, jax.numpy as jnp
from jax import lax
from jax.experimental import pallas as pl
from jax.experimental.pallas import tpu as pltpu
from jax.sharding import PartitionSpec as P

F32 = jnp.float32
BF16 = jnp.bfloat16
NEG_BIG = -1e30
TILE = 256
WIDE = 512
VMEM_BYTES = 32 * 2**20


def mm(left, right):
    return jnp.dot(left, right, preferred_element_type=F32)


def fold(tile):
    return tile.reshape(tile.shape[0] // 8, 8, tile.shape[1])


def token_of(shape, tokens):
    return lax.rem(lax.broadcasted_iota(jnp.int32, shape, 1), tokens)


def causal(scores, tokens, length):
    key = lax.broadcasted_iota(jnp.int32, scores.shape, 0)
    return jnp.where((key <= token_of(scores.shape, tokens)) & (key < length), scores, NEG_BIG)


def parts_of(ref):
    return [slice(i, i + WIDE) for i in range(0, ref.shape[1], WIDE)]


def call(body, out_shape, scratch, name, *args):
    specs = [
        pl.BlockSpec(memory_space=pltpu.SMEM if a.ndim == 1 else pltpu.VMEM) for a in args
    ]
    return pl.pallas_call(
        body,
        in_specs=specs,
        out_specs=[pl.BlockSpec(memory_space=pltpu.VMEM)] * len(out_shape),
        out_shape=[jax.ShapeDtypeStruct(s, d) for s, d in out_shape],
        scratch_shapes=scratch,
        compiler_params=pltpu.CompilerParams(vmem_limit_bytes=VMEM_BYTES),
        name=name,
    )(*args)


def arrange(length, queries, grads, mask):
    tokens, width = queries.shape
    head = 128
    heads = width // head

    def body(length_ref, q_ref, g_ref, mask_ref, qt_ref, gt_ref, q_rows_ref, g_rows_ref):
        kept = (token_of((1, tokens), tokens) < length_ref[0]) & (mask_ref[...] == 1)
        for h in range(heads):
            cols, rows = slice(h * head, (h + 1) * head), slice(h * tokens, (h + 1) * tokens)
            q = q_ref[:, cols]
            q_rows_ref[rows, :] = q
            qt_ref[:, rows] = q.T
            gt = jnp.where(kept, g_ref[:, cols].T, jnp.zeros((), BF16))
            gt_ref[:, rows] = gt
            g_rows_ref[rows, :] = gt.T

    down, across = ((heads * tokens, head), BF16), ((head, heads * tokens), BF16)
    return call(body, [across, across, down, down], [], "arrange", length, queries, grads, mask)


def forward(qt, keys_values, state, own=None, last=None):
    head, wide = qt.shape
    n = len(keys_values)
    rows = keys_values[0][0].shape[0]
    factor = head ** (-0.5) * math.log2(math.e)
    tiles = [(j, i) for j in range(n) for i in range(0, rows, TILE)]

    def body(*refs):
        refs = list(refs)
        length = refs.pop(0)[0] if own or last else None
        qt_ref = refs.pop(0)
        gt_ref = refs.pop(0) if last else None
        kv = [(refs.pop(0), refs.pop(0)) if own else (refs.pop(0),) for _ in range(n)]
        if state is not None:
            old_stat, old_sum = refs.pop(0), refs.pop(0)
        stat_ref, sum_ref, score_ref = refs
        if own:
            keys = [kv[0][0][...]]
            vt = kv[0][1][...].T
        else:
            keys = [kv[j][0][i : i + TILE, :head] for j, i in tiles]
            vt = jnp.concatenate([r[0][:, head:].T for r in kv], axis=1)
        for part in parts_of(qt_ref):
            high = None
            for i, k in enumerate(keys):
                scores = mm(k, qt_ref[:, part])
                if own:
                    scores = causal(scores, own[1], length)
                score_ref[i * TILE : (i + 1) * TILE, part] = scores
                peak = jnp.max(fold(scores), axis=0)
                high = peak if high is None else jnp.maximum(high, peak)
            top = jnp.max(high, axis=0, keepdims=True)
            if state is not None:
                before = old_stat[0:1, part]
                top = jnp.maximum(top, before)
            total, summed = None, None
            for i in range(len(keys)):
                weights = jnp.exp2((score_ref[i * TILE : (i + 1) * TILE, part] - top) * factor)
                here = jnp.sum(fold(weights), axis=0)
                total = here if total is None else total + here
                here = mm(vt[:, i * TILE : (i + 1) * TILE], weights.astype(BF16))
                summed = here if summed is None else summed + here
            total = jnp.sum(total, axis=0, keepdims=True)
            if state is not None:
                keep = jnp.exp2((before - top) * factor)
                total = total + keep * old_stat[1:2, part]
                summed = summed + keep * old_sum[:, part]
            if last:
                alive = token_of((1, WIDE), last[1]) < length
                attended = jnp.where(alive, summed / total, 0.0).astype(BF16)
                inner = gt_ref[:, part].astype(F32) * attended.astype(F32)
                stat_ref[0:1, part] = top * factor + jnp.log2(total)
                stat_ref[1:2, part] = jnp.sum(inner, axis=0, keepdims=True)
                sum_ref[:, part] = attended
            else:
                stat_ref[0:1, part] = top
                stat_ref[1:2, part] = total
                sum_ref[:, part] = summed

    args = [own[0], qt] if own else [last[0], qt, last[2]] if last else [qt]
    for x in keys_values:
        args += list(x)
    args += [] if state is None else list(state)
    return call(
        body,
        [((8, wide), F32), ((head, wide), BF16 if last else F32)],
        [pltpu.VMEM((n * rows, wide), F32)],
        "forward",
        *args,
    )


def probabilities(scores, pgrad, back_ref, part, factor):
    prob = jnp.exp2(scores * factor - back_ref[0:1, part])
    return prob.astype(BF16), (prob * (pgrad - back_ref[1:2, part])).astype(BF16)


def backward(arranged, back, planes):
    qt, gt, q_rows, g_rows = arranged
    head, wide = qt.shape
    n = len(planes)
    rows = planes[0].shape[0]
    scale = head ** (-0.5)
    factor = scale * math.log2(math.e)

    def body(*refs):
        qt_ref, gt_ref, q_rows_ref, g_rows_ref, back_ref = refs[:5]
        planes_in, terms, dscores, prob_ref = refs[5 : 5 + n], refs[5 + n : 5 + 2 * n], refs[5 + 2 * n : 5 + 3 * n], refs[-1]
        for j in range(n):
            for part in parts_of(qt_ref):
                for i in range(0, rows, TILE):
                    here = slice(i, i + TILE)
                    scores = mm(planes_in[j][here, :head], qt_ref[:, part])
                    pgrad = mm(planes_in[j][here, head:], gt_ref[:, part])
                    prob, dscore = probabilities(scores, pgrad, back_ref, part, factor)
                    prob_ref[here, part] = prob
                    dscores[j][here, part] = dscore
            for i in range(0, rows, TILE):
                here = slice(i, i + TILE)
                terms[j][here, :head] = (mm(dscores[j][here, :], q_rows_ref[...]) * scale).astype(BF16)
                terms[j][here, head:] = mm(prob_ref[here, :], g_rows_ref[...]).astype(BF16)

    out = call(
        body,
        [(x.shape, BF16) for x in planes] + [((rows, wide), BF16)] * n,
        [pltpu.VMEM((rows, wide), BF16)],
        "backward",
        qt, gt, q_rows, g_rows, back, *planes,
    )
    return out[:n], out[n:]


def lay_out(attended, planes, dscores, tokens):
    head, wide = attended.shape
    n = len(planes)

    def body(*refs):
        att_ref, planes_in, dscores_in, (out_ref, dq_ref) = refs[0], refs[1 : 1 + n], refs[1 + n : 1 + 2 * n], refs[-2:]
        kt = [x[:, :head].T for x in planes_in]
        for part in parts_of(att_ref):
            total = None
            for k, d in zip(kt, dscores_in):
                add = mm(k, d[:, part])
                total = add if total is None else total + add
            dq_ref[:, part] = total
        for h in range(wide // tokens):
            out_ref[:, h * head : (h + 1) * head] = att_ref[:, h * tokens : (h + 1) * tokens].T

    return call(
        body, [((tokens, wide // tokens * head), BF16), ((head, wide), F32)], [], "lay_out", attended, *planes, *dscores
    )


def backward_own(length, arranged, back, keys, values, dq, plane, plane_dscore):
    qt, gt, q_rows, g_rows = arranged
    head, wide = qt.shape
    tokens = keys.shape[0]
    scale = head ** (-0.5)
    factor = scale * math.log2(math.e)

    def body(
        length_ref, qt_ref, gt_ref, q_rows_ref, g_rows_ref, back_ref, k_ref, v_ref, old_dq, plane_ref, plane_dscore_ref,
        dq_ref, dk_ref, dv_ref, prob_ref, dscore_ref,
    ):
        kt = k_ref[...].T
        plane_kt = plane_ref[:, :head].T
        for part in parts_of(qt_ref):
            scores = causal(mm(k_ref[...], qt_ref[:, part]), tokens, length_ref[0])
            pgrad = mm(v_ref[...], gt_ref[:, part])
            prob, dscore = probabilities(scores, pgrad, back_ref, part, factor)
            prob_ref[:, part] = prob
            dscore_ref[:, part] = dscore
            total = old_dq[:, part] + mm(kt, dscore) + mm(plane_kt, plane_dscore_ref[:, part])
            out = (total * scale).astype(BF16)
            for i in range(WIDE // tokens):
                h = part.start // tokens + i
                dq_ref[:, h * head : (h + 1) * head] = out[:, i * tokens : (i + 1) * tokens].T
        dk_ref[...] = (mm(dscore_ref[...], q_rows_ref[...]) * scale).astype(BF16)
        dv_ref[...] = mm(prob_ref[...], g_rows_ref[...]).astype(BF16)

    return call(
        body,
        [((tokens, wide // tokens * head), BF16), (keys.shape, BF16), (values.shape, BF16)],
        [pltpu.VMEM((tokens, wide), BF16), pltpu.VMEM((tokens, wide), BF16)],
        "backward_own",
        length, qt, gt, q_rows, g_rows, back, keys, values, dq, plane, plane_dscore,
    )


def collect(parts, head):
    def body(in_ref, key_ref, value_ref):
        total = jnp.sum(in_ref[...].astype(F32), axis=0).astype(BF16)
        key_ref[...] = total[:, :head]
        value_ref[...] = total[:, head:]

    shape = ((parts.shape[1], head), BF16)
    return call(body, [shape, shape], [], "collect", parts)


Z_SIZE = 8


def shards(queries, resp_keys, resp_values, prefix_keys, prefix_values, out_grad, lengths, loss_mask):
    group_count = lax.axis_size("grp")
    z_size = Z_SIZE
    y_size = group_count // z_size
    z_groups = [[y * z_size + z for z in range(z_size)] for y in range(y_size)]

    def along_y(x, shift):
        pairs = [(y * z_size + z, (y + shift) % y_size * z_size + z) for y in range(y_size) for z in range(z_size)]
        return lax.ppermute(x, "grp", pairs)

    def along_z(x):
        return lax.all_to_all(x, "grp", 0, 0, axis_index_groups=z_groups, tiled=True)

    length = lax.dynamic_slice_in_dim(lengths, lax.axis_index("grp"), 1, 0)
    own_keys, own_values = resp_keys[0], resp_values[0]
    tokens = own_keys.shape[0]
    block = jnp.concatenate([prefix_keys, prefix_values], axis=1)
    rows, width = block.shape
    head = width // 2
    mine = along_z(jnp.broadcast_to(block[None], (z_size, rows, width))).reshape(z_size * rows, width)
    arranged = arrange(length, queries[0], out_grad[0], loss_mask)
    qt, gt = arranged[:2]
    state = forward(qt, [(own_keys, own_values)], None, own=(length, tokens))
    mine, state = lax.optimization_barrier((mine, state))
    near, other, far = along_y(mine, 1), along_y(mine, 3), along_y(mine, 2)
    state = forward(qt, [(mine,)], state)
    state = forward(qt, [(near,), (other,)], state)
    back, attended = forward(qt, [(far,)], state, last=(length, tokens, gt))
    (far_terms,), (far_ds,) = backward(arranged, back, [far])
    far_terms = along_y(far_terms, 2)
    (near_terms, other_terms), (near_ds, other_ds) = backward(arranged, back, [near, other])
    near_terms, other_terms = along_y(near_terms, 3), along_y(other_terms, 1)
    held, far_terms = lax.optimization_barrier((mine, far_terms))
    (mine_terms,), (mine_ds,) = backward(arranged, back, [held])
    attended, dq = lay_out(attended, [near, other, far], [near_ds, other_ds, far_ds], tokens)
    mine_terms, attended, dq = lax.optimization_barrier((mine_terms, attended, dq))
    part = sum(x.astype(F32) for x in (mine_terms, near_terms, other_terms, far_terms)).astype(BF16)
    part = along_z(part.reshape(z_size, rows, width))
    query_grad, key_grad, value_grad = backward_own(
        length, arranged, back, own_keys, own_values, dq, mine, mine_ds
    )
    key_share, value_share = collect(part, head)
    return (attended[None], query_grad[None], key_grad[None], value_grad[None], key_share, value_share)


def solution(mesh):
    placed = (
        P(("prompt", "grp"), None, None),
        P(("prompt", "grp"), None, None),
        P(("prompt", "grp"), None, None),
        P(("prompt", "grp"), None),
        P(("prompt", "grp"), None),
        P(("prompt", "grp"), None, None),
        P("prompt"),
        P(("prompt", "grp"), None),
    )
    return jax.shard_map(
        shards,
        mesh=mesh,
        in_specs=placed,
        out_specs=(
            P(("prompt", "grp"), None, None),
            P(("prompt", "grp"), None, None),
            P(("prompt", "grp"), None, None),
            P(("prompt", "grp"), None, None),
            P(("prompt", "grp"), None),
            P(("prompt", "grp"), None),
        ),
        check_vma=False,
    )
```

```python
import math
import jax, jax.numpy as jnp
from jax import lax
from jax.experimental import pallas as pl
from jax.experimental.pallas import tpu as pltpu
from jax.sharding import PartitionSpec as P

F32 = jnp.float32
BF16 = jnp.bfloat16
NEG_BIG = -1e30
TILE = 256
WIDE = 512
VMEM_BYTES = 14 * 2**20
ALL_VMEM_BYTES = 57 * 2**20


def mm(left, right):
    return jnp.dot(left, right, preferred_element_type=F32)


def fold(tile):
    return tile.reshape(tile.shape[0] // 8, 8, tile.shape[1])


def token_of(shape, tokens):
    return lax.rem(lax.broadcasted_iota(jnp.int32, shape, 1), tokens)


def causal(scores, tokens, length):
    key = lax.broadcasted_iota(jnp.int32, scores.shape, 0)
    return jnp.where((key <= token_of(scores.shape, tokens)) & (key < length), scores, NEG_BIG)


def own_length(lengths_ref):
    return lengths_ref[lax.axis_index("grp")]


def parts_of(ref):
    return [slice(i, i + WIDE) for i in range(0, ref.shape[1], WIDE)]


def call(body, out_shape, scratch, name, *args, space=pltpu.VMEM, limit=VMEM_BYTES):
    specs = [pl.BlockSpec(memory_space=pltpu.SMEM if a.ndim == 1 else space) for a in args]
    return pl.pallas_call(
        body,
        in_specs=specs,
        out_specs=[pl.BlockSpec(memory_space=pltpu.VMEM)] * len(out_shape),
        out_shape=[jax.ShapeDtypeStruct(s, d) for s, d in out_shape],
        scratch_shapes=scratch,
        compiler_params=pltpu.CompilerParams(vmem_limit_bytes=limit),
        name=name,
    )(*args)


def emit_scores(keys, qt_ref, score_ref, mask):
    highs = []
    for part in parts_of(qt_ref):
        high = None
        for i, k in enumerate(keys):
            scores = mask(mm(k, qt_ref[:, part]))
            score_ref[i * TILE : (i + 1) * TILE, part] = scores
            peak = jnp.max(fold(scores), axis=0)
            high = peak if high is None else jnp.maximum(high, peak)
        highs.append(high)
    return highs


def emit_sums(n, top, vt, score_ref, part, factor):
    total, summed = None, None
    for i in range(n):
        weights = jnp.exp2((score_ref[i * TILE : (i + 1) * TILE, part] - top) * factor)
        here = jnp.sum(fold(weights), axis=0)
        total = here if total is None else total + here
        here = mm(vt[:, i * TILE : (i + 1) * TILE], weights.astype(BF16))
        summed = here if summed is None else summed + here
    return jnp.sum(total, axis=0, keepdims=True), summed


def start(lengths, queries, grads, mask, keys, values):
    tokens, width = queries.shape
    head = keys.shape[1]
    heads = width // head
    wide = heads * tokens
    factor = head ** (-0.5) * math.log2(math.e)

    def body(
        lengths_ref, q_in, g_in, mask_in, k_in, v_in,
        qt_ref, gt_ref, q_rows_ref, g_rows_ref, stat_ref, sum_ref,
        q_ref, g_ref, mask_ref, k_ref, v_ref, score_ref, sems,
    ):
        copies = [
            pltpu.make_async_copy(a, b, sems.at[i])
            for i, (a, b) in enumerate(
                [(q_in, q_ref), (k_in, k_ref), (v_in, v_ref), (mask_in, mask_ref), (g_in, g_ref)]
            )
        ]
        for c in copies:
            c.start()
        length = own_length(lengths_ref)
        copies[0].wait()
        for h in range(heads):
            cols, rows = slice(h * head, (h + 1) * head), slice(h * tokens, (h + 1) * tokens)
            q = q_ref[:, cols]
            q_rows_ref[rows, :] = q
            qt_ref[:, rows] = q.T
        copies[1].wait()
        copies[2].wait()
        highs = emit_scores([k_ref[...]], qt_ref, score_ref, lambda s: causal(s, tokens, length))
        vt = v_ref[...].T
        for part, high in zip(parts_of(qt_ref), highs):
            top = jnp.max(high, axis=0, keepdims=True)
            total, summed = emit_sums(1, top, vt, score_ref, part, factor)
            stat_ref[0:1, part] = top
            stat_ref[1:2, part] = total
            sum_ref[:, part] = summed
        copies[3].wait()
        copies[4].wait()
        kept = (token_of((1, tokens), tokens) < length) & (mask_ref[...] == 1)
        for h in range(heads):
            cols, rows = slice(h * head, (h + 1) * head), slice(h * tokens, (h + 1) * tokens)
            gt = jnp.where(kept, g_ref[:, cols].T, jnp.zeros((), BF16))
            gt_ref[:, rows] = gt
            g_rows_ref[rows, :] = gt.T

    down, across = ((wide, head), BF16), ((head, wide), BF16)
    args = [queries, grads, mask, keys, values]
    return call(
        body,
        [across, across, down, down, ((8, wide), F32), ((head, wide), F32)],
        [pltpu.VMEM(x.shape, x.dtype) for x in args]
        + [pltpu.VMEM((tokens, wide), F32), pltpu.SemaphoreType.DMA((5,))],
        "start",
        lengths,
        *args,
        space=pltpu.HBM,
        limit=ALL_VMEM_BYTES,
    )


def emit_pgrads(values, gt_ref, pgrad_ref):
    for part in parts_of(gt_ref):
        for i, v in enumerate(values):
            pgrad_ref[i * TILE : (i + 1) * TILE, part] = mm(v, gt_ref[:, part])


def merge(old_stat, old_sum, part, high, n, vt, score_ref, factor):
    before = old_stat[0:1, part]
    top = jnp.maximum(jnp.max(high, axis=0, keepdims=True), before)
    total, summed = emit_sums(n, top, vt, score_ref, part, factor)
    keep = jnp.exp2((before - top) * factor)
    return top, total + keep * old_stat[1:2, part], summed + keep * old_sum[:, part]


def probabilities(scores, pgrad, back_ref, part, factor):
    prob = jnp.exp2(scores * factor - back_ref[0:1, part])
    return prob.astype(BF16), (prob * (pgrad - back_ref[1:2, part])).astype(BF16)


def emit_dscores(score_ref, pgrad_ref, back_ref, prob_ref, dscore_ref, factor):
    for part in parts_of(score_ref):
        for i in range(0, score_ref.shape[0], TILE):
            here = slice(i, i + TILE)
            prob, dscore = probabilities(score_ref[here, part], pgrad_ref[here, part], back_ref, part, factor)
            prob_ref[here, part] = prob
            dscore_ref[here, part] = dscore


def emit_terms(prob_ref, dscore_ref, q_rows_ref, g_rows_ref, terms_ref, scale):
    head = q_rows_ref.shape[1]
    for i in range(0, prob_ref.shape[0], TILE):
        here = slice(i, i + TILE)
        terms_ref[here, :head] = (mm(dscore_ref[here, :], q_rows_ref[...]) * scale).astype(BF16)
        terms_ref[here, head:] = mm(prob_ref[here, :], g_rows_ref[...]).astype(BF16)


def split(planes_in, head):
    keys = [x[i : i + TILE, :head] for x in planes_in for i in range(0, x.shape[0], TILE)]
    values = [x[i : i + TILE, head:] for x in planes_in for i in range(0, x.shape[0], TILE)]
    vt = jnp.concatenate([x[:, head:].T for x in planes_in], axis=1)
    return keys, values, vt


def forward(qt, gt, planes, state):
    head, wide = qt.shape
    n = len(planes)
    rows = planes[0].shape[0]
    factor = head ** (-0.5) * math.log2(math.e)

    def body(*refs):
        qt_ref, gt_ref = refs[:2]
        old_stat, old_sum, stat_ref, sum_ref, score_ref, pgrad_ref = refs[2 + n :]
        keys, values, vt = split(refs[2 : 2 + n], head)
        highs = emit_scores(keys, qt_ref, score_ref, lambda s: s)
        for part, high in zip(parts_of(qt_ref), highs):
            top, total, summed = merge(old_stat, old_sum, part, high, len(keys), vt, score_ref, factor)
            stat_ref[0:1, part] = top
            stat_ref[1:2, part] = total
            sum_ref[:, part] = summed
        emit_pgrads(values, gt_ref, pgrad_ref)

    kept = ((n * rows, wide), F32)
    stat, summed, scores, pgrads = call(
        body, [((8, wide), F32), ((head, wide), F32), kept, kept], [], "forward", qt, gt, *planes, *state
    )
    return (stat, summed), (scores, pgrads)


def turn(lengths, arranged, planes, state, tokens):
    qt, gt, q_rows, g_rows = arranged
    head, wide = qt.shape
    n = len(planes)
    rows = n * planes[0].shape[0]
    scale = head ** (-0.5)
    factor = scale * math.log2(math.e)

    def body(*refs):
        lengths_ref, qt_ref, gt_ref, q_rows_ref, g_rows_ref = refs[:5]
        old_stat, old_sum, back_ref, att_ref, terms_ref, dscore_ref, score_ref, pgrad_ref, prob_ref = refs[5 + n :]
        length = own_length(lengths_ref)
        keys, values, vt = split(refs[5 : 5 + n], head)
        highs = emit_scores(keys, qt_ref, score_ref, lambda s: s)
        emit_pgrads(values, gt_ref, pgrad_ref)
        alive = token_of((1, WIDE), tokens) < length
        for part, high in zip(parts_of(qt_ref), highs):
            top, total, summed = merge(old_stat, old_sum, part, high, len(keys), vt, score_ref, factor)
            attended = jnp.where(alive, summed / total, 0.0).astype(BF16)
            inner = gt_ref[:, part].astype(F32) * attended.astype(F32)
            back_ref[0:1, part] = top * factor + jnp.log2(total)
            back_ref[1:2, part] = jnp.sum(inner, axis=0, keepdims=True)
            att_ref[:, part] = attended
        emit_dscores(score_ref, pgrad_ref, back_ref, prob_ref, dscore_ref, factor)
        emit_terms(prob_ref, dscore_ref, q_rows_ref, g_rows_ref, terms_ref, scale)

    return call(
        body,
        [((8, wide), F32), ((head, wide), BF16), ((rows, 2 * head), BF16), ((rows, wide), BF16)],
        [pltpu.VMEM((rows, wide), F32), pltpu.VMEM((rows, wide), F32), pltpu.VMEM((rows, wide), BF16)],
        "turn",
        lengths, qt, gt, q_rows, g_rows, *planes, *state,
    )


def backward(arranged, back, kept, n):
    q_rows, g_rows = arranged[2:]
    wide, head = q_rows.shape
    rows = kept[0].shape[0] // n
    scale = head ** (-0.5)
    factor = scale * math.log2(math.e)

    def body(*refs):
        q_rows_ref, g_rows_ref, back_ref, score_ref, pgrad_ref = refs[:5]
        terms, dscores, prob_ref = refs[5 : 5 + n], refs[5 + n : 5 + 2 * n], refs[-1]
        for j in range(n):
            here = slice(j * rows, (j + 1) * rows)
            emit_dscores(
                score_ref.at[here, :], pgrad_ref.at[here, :], back_ref, prob_ref.at[here, :], dscores[j], factor
            )
            emit_terms(prob_ref.at[here, :], dscores[j], q_rows_ref, g_rows_ref, terms[j], scale)

    out = call(
        body,
        [((rows, 2 * head), BF16)] * n + [((rows, wide), BF16)] * n,
        [pltpu.VMEM((n * rows, wide), BF16)],
        "backward",
        q_rows, g_rows, back, *kept,
    )
    return out[:n], out[n:]


def finish(lengths, arranged, back, keys, values, attended, planes, dscores):
    qt, gt, q_rows, g_rows = arranged
    head, wide = qt.shape
    tokens = keys.shape[0]
    n = len(planes)
    scale = head ** (-0.5)
    factor = scale * math.log2(math.e)

    def body(*refs):
        lengths_ref, qt_ref, gt_ref, q_rows_ref, g_rows_ref, back_ref, k_ref, v_ref, att_ref = refs[:9]
        planes_in, dscores_in = refs[9 : 9 + n], refs[9 + n : -6]
        out_ref, dq_ref, dk_ref, dv_ref, prob_ref, dscore_ref = refs[-6:]
        length = own_length(lengths_ref)
        kt = k_ref[...].T
        kts, planes_kt = [x[:, :head].T for x in planes_in], []
        for d in dscores_in:
            group = [kts.pop(0)]
            while sum(k.shape[1] for k in group) < d.shape[0]:
                group.append(kts.pop(0))
            planes_kt.append(jnp.concatenate(group, axis=1))
        for part in parts_of(qt_ref):
            scores = causal(mm(k_ref[...], qt_ref[:, part]), tokens, length)
            pgrad = mm(v_ref[...], gt_ref[:, part])
            prob, dscore = probabilities(scores, pgrad, back_ref, part, factor)
            prob_ref[:, part] = prob
            dscore_ref[:, part] = dscore
            total = mm(kt, dscore)
            for k, d in zip(planes_kt, dscores_in):
                total = total + mm(k, d[:, part])
            out = (total * scale).astype(BF16)
            for i in range(WIDE // tokens):
                h = part.start // tokens + i
                dq_ref[:, h * head : (h + 1) * head] = out[:, i * tokens : (i + 1) * tokens].T
                out_ref[:, h * head : (h + 1) * head] = att_ref[:, h * tokens : (h + 1) * tokens].T
        dk_ref[...] = (mm(dscore_ref[...], q_rows_ref[...]) * scale).astype(BF16)
        dv_ref[...] = mm(prob_ref[...], g_rows_ref[...]).astype(BF16)

    flat = ((tokens, wide // tokens * head), BF16)
    return call(
        body,
        [flat, flat, (keys.shape, BF16), (values.shape, BF16)],
        [pltpu.VMEM((tokens, wide), BF16), pltpu.VMEM((tokens, wide), BF16)],
        "finish",
        lengths, qt, gt, q_rows, g_rows, back, keys, values, attended, *planes, *dscores,
    )


def spread(keys, values, count):
    rows, head = keys.shape

    def body(k_ref, v_ref, out_ref):
        for i in range(count):
            out_ref[i, :, :head] = k_ref[...]
            out_ref[i, :, head:] = v_ref[...]

    return call(body, [((count, rows, 2 * head), BF16)], [], "spread", keys, values, limit=ALL_VMEM_BYTES)[0]


def collect(parts, head):
    def body(in_ref, key_ref, value_ref):
        total = jnp.sum(in_ref[...].astype(F32), axis=0).astype(BF16)
        key_ref[...] = total[:, :head]
        value_ref[...] = total[:, head:]

    shape = ((parts.shape[1], head), BF16)
    return call(body, [shape, shape], [], "collect", parts)


Z_SIZE = 8


def shards(queries, resp_keys, resp_values, prefix_keys, prefix_values, out_grad, lengths, loss_mask):
    group_count = lax.axis_size("grp")
    z_size = Z_SIZE
    y_size = group_count // z_size
    z_groups = [[y * z_size + z for z in range(z_size)] for y in range(y_size)]

    def along_y(x, shift):
        pairs = [(y * z_size + z, (y + shift) % y_size * z_size + z) for y in range(y_size) for z in range(z_size)]
        return lax.ppermute(x, "grp", pairs)

    def along_z(x):
        return lax.all_to_all(x, "grp", 0, 0, axis_index_groups=z_groups, tiled=True)

    own_keys, own_values = resp_keys[0], resp_values[0]
    tokens = own_keys.shape[0]
    rows, head = prefix_keys.shape
    mine = along_z(spread(prefix_keys, prefix_values, z_size)).reshape(z_size * rows, 2 * head)
    *arranged, stat, summed = start(lengths, queries[0], out_grad[0], loss_mask, own_keys, own_values)
    qt, gt = arranged[:2]
    mine, stat, summed = lax.optimization_barrier((mine, stat, summed))
    near, other = along_y(mine, 1), along_y(mine, 3)
    state, mine_kept = forward(qt, gt, [mine], (stat, summed))
    near, other, *state = lax.optimization_barrier((near, other, *state))
    half = mine.shape[0] // 2
    far = [along_y(near[:half], 1), along_y(other[half:], 3)]
    state, kept = forward(qt, gt, [near, other], state)
    back, attended, far_terms, far_ds = turn(lengths, arranged, far, state, tokens)
    far_terms = along_y(far_terms, 2)
    (near_terms, other_terms), (near_ds, other_ds) = backward(arranged, back, kept, 2)
    near_terms, other_terms = along_y(near_terms, 3), along_y(other_terms, 1)
    held, far_terms = lax.optimization_barrier((back, far_terms))
    (mine_terms,), (mine_ds,) = backward(arranged, held, mine_kept, 1)
    attended, query_grad, key_grad, value_grad = finish(
        lengths, arranged, back, own_keys, own_values, attended,
        [mine, near, other, *far], [mine_ds, near_ds, other_ds, far_ds],
    )
    mine_terms, attended, query_grad, key_grad, value_grad = lax.optimization_barrier(
        (mine_terms, attended, query_grad, key_grad, value_grad)
    )
    part = sum(x.astype(F32) for x in (mine_terms, near_terms, other_terms, far_terms)).astype(BF16)
    key_share, value_share = collect(along_z(part.reshape(z_size, rows, 2 * head)), head)
    return (attended[None], query_grad[None], key_grad[None], value_grad[None], key_share, value_share)


def solution(mesh):
    placed = (
        P(("prompt", "grp"), None, None),
        P(("prompt", "grp"), None, None),
        P(("prompt", "grp"), None, None),
        P(("prompt", "grp"), None),
        P(("prompt", "grp"), None),
        P(("prompt", "grp"), None, None),
        P("prompt"),
        P(("prompt", "grp"), None),
    )
    return jax.shard_map(
        shards,
        mesh=mesh,
        in_specs=placed,
        out_specs=(
            P(("prompt", "grp"), None, None),
            P(("prompt", "grp"), None, None),
            P(("prompt", "grp"), None, None),
            P(("prompt", "grp"), None, None),
            P(("prompt", "grp"), None),
            P(("prompt", "grp"), None),
        ),
        check_vma=False,
    )
```

```python
import math
import jax, jax.numpy as jnp
from jax import lax
from jax.experimental import pallas as pl
from jax.experimental.pallas import tpu as pltpu
from jax.sharding import PartitionSpec as P

F32 = jnp.float32
BF16 = jnp.bfloat16
NEG_BIG = -1e30
TILE = 256
WIDE = 512
VMEM_BYTES = 14 * 2**20
ALL_VMEM_BYTES = 57 * 2**20


def mm(left, right):
    return jnp.dot(left, right, preferred_element_type=F32)


def fold(tile):
    return tile.reshape(tile.shape[0] // 8, 8, tile.shape[1])


def token_of(shape, tokens):
    return lax.rem(lax.broadcasted_iota(jnp.int32, shape, 1), tokens)


def causal(scores, tokens, length):
    key = lax.broadcasted_iota(jnp.int32, scores.shape, 0)
    return jnp.where((key <= token_of(scores.shape, tokens)) & (key < length), scores, NEG_BIG)


def own_length(lengths_ref):
    return lengths_ref[lax.axis_index("grp")]


def parts_of(ref):
    return [slice(i, i + WIDE) for i in range(0, ref.shape[1], WIDE)]


def call(body, out_shape, scratch, name, *args, space=pltpu.VMEM, limit=VMEM_BYTES):
    specs = [pl.BlockSpec(memory_space=pltpu.SMEM if a.ndim == 1 else space) for a in args]
    return pl.pallas_call(
        body,
        in_specs=specs,
        out_specs=[pl.BlockSpec(memory_space=pltpu.VMEM)] * len(out_shape),
        out_shape=[jax.ShapeDtypeStruct(s, d) for s, d in out_shape],
        scratch_shapes=scratch,
        compiler_params=pltpu.CompilerParams(vmem_limit_bytes=limit),
        name=name,
    )(*args)


def put_state(state_ref, part, top, total, summed):
    head = state_ref.shape[0] - 8
    state_ref[:head, part] = summed
    state_ref[head : head + 1, part] = top
    state_ref[head + 1 : head + 2, part] = total


def emit_scores(keys, qt_ref, score_ref, mask):
    highs = []
    for part in parts_of(qt_ref):
        high = None
        for i, k in enumerate(keys):
            scores = mask(mm(k, qt_ref[:, part]))
            score_ref[i * TILE : (i + 1) * TILE, part] = scores
            peak = jnp.max(fold(scores), axis=0)
            high = peak if high is None else jnp.maximum(high, peak)
        highs.append(high)
    return highs


def emit_sums(n, top, vt, score_ref, part, factor):
    total, summed = None, None
    for i in range(n):
        weights = jnp.exp2((score_ref[i * TILE : (i + 1) * TILE, part] - top) * factor)
        here = jnp.sum(fold(weights), axis=0)
        total = here if total is None else total + here
        here = mm(vt[:, i * TILE : (i + 1) * TILE], weights.astype(BF16))
        summed = here if summed is None else summed + here
    return jnp.sum(total, axis=0, keepdims=True), summed


def start(lengths, queries, grads, mask, keys, values):
    tokens, width = queries.shape
    head = keys.shape[1]
    heads = width // head
    wide = heads * tokens
    factor = head ** (-0.5) * math.log2(math.e)

    def body(
        lengths_ref, q_in, g_in, mask_in, k_in, v_in,
        across_ref, down_ref, state_ref,
        q_ref, g_ref, mask_ref, k_ref, v_ref, score_ref, sems,
    ):
        copies = [
            pltpu.make_async_copy(a, b, sems.at[i])
            for i, (a, b) in enumerate(
                [(q_in, q_ref), (k_in, k_ref), (v_in, v_ref), (mask_in, mask_ref), (g_in, g_ref)]
            )
        ]
        for c in copies:
            c.start()
        length = own_length(lengths_ref)
        qt_ref, gt_ref = across_ref.at[:head, :], across_ref.at[head:, :]
        copies[0].wait()
        for h in range(heads):
            cols, rows = slice(h * head, (h + 1) * head), slice(h * tokens, (h + 1) * tokens)
            q = q_ref[:, cols]
            down_ref[rows, :head] = q
            qt_ref[:, rows] = q.T
        copies[1].wait()
        copies[2].wait()
        highs = emit_scores([k_ref[...]], qt_ref, score_ref, lambda s: causal(s, tokens, length))
        vt = v_ref[...].T
        for part, high in zip(parts_of(qt_ref), highs):
            top = jnp.max(high, axis=0, keepdims=True)
            total, summed = emit_sums(1, top, vt, score_ref, part, factor)
            put_state(state_ref, part, top, total, summed)
        copies[3].wait()
        copies[4].wait()
        kept = (token_of((1, tokens), tokens) < length) & (mask_ref[...] == 1)
        for h in range(heads):
            cols, rows = slice(h * head, (h + 1) * head), slice(h * tokens, (h + 1) * tokens)
            gt = jnp.where(kept, g_ref[:, cols].T, jnp.zeros((), BF16))
            gt_ref[:, rows] = gt
            down_ref[rows, head:] = gt.T

    args = [queries, grads, mask, keys, values]
    return call(
        body,
        [((2 * head, wide), BF16), ((wide, 2 * head), BF16), ((head + 8, wide), F32)],
        [pltpu.VMEM(x.shape, x.dtype) for x in args]
        + [pltpu.VMEM((tokens, wide), F32), pltpu.SemaphoreType.DMA((5,))],
        "start",
        lengths,
        *args,
        space=pltpu.HBM,
        limit=ALL_VMEM_BYTES,
    )


def emit_pgrads(values, gt_ref, pgrad_ref):
    for part in parts_of(gt_ref):
        for i, v in enumerate(values):
            pgrad_ref[i * TILE : (i + 1) * TILE, part] = mm(v, gt_ref[:, part])


def merge(state_ref, part, high, n, vt, score_ref, factor):
    head = state_ref.shape[0] - 8
    before = state_ref[head : head + 1, part]
    top = jnp.maximum(jnp.max(high, axis=0, keepdims=True), before)
    total, summed = emit_sums(n, top, vt, score_ref, part, factor)
    keep = jnp.exp2((before - top) * factor)
    return top, total + keep * state_ref[head + 1 : head + 2, part], summed + keep * state_ref[:head, part]


def probabilities(scores, pgrad, back_ref, part, factor):
    prob = jnp.exp2(scores * factor - back_ref[0:1, part])
    return prob.astype(BF16), (prob * (pgrad - back_ref[1:2, part])).astype(BF16)


def emit_dscores(score_ref, pgrad, back_ref, prob_ref, dscore_ref, factor):
    for part in parts_of(score_ref):
        for i in range(score_ref.shape[0] // TILE):
            here = slice(i * TILE, (i + 1) * TILE)
            prob, dscore = probabilities(score_ref[here, part], pgrad(i, part), back_ref, part, factor)
            prob_ref[here, part] = prob
            dscore_ref[here, part] = dscore


def emit_terms(prob_ref, dscore_ref, down_ref, terms_ref, scale):
    head = down_ref.shape[1] // 2
    for i in range(0, prob_ref.shape[0], TILE):
        here = slice(i, i + TILE)
        terms_ref[here, :head] = (mm(dscore_ref[here, :], down_ref[:, :head]) * scale).astype(BF16)
        terms_ref[here, head:] = mm(prob_ref[here, :], down_ref[:, head:]).astype(BF16)


def split(planes_in, head):
    keys = [x[i : i + TILE, :head] for x in planes_in for i in range(0, x.shape[0], TILE)]
    values = [x[i : i + TILE, head:] for x in planes_in for i in range(0, x.shape[0], TILE)]
    vt = jnp.concatenate([x[:, head:].T for x in planes_in], axis=1)
    return keys, values, vt


def forward(across, planes, state):
    head, wide = across.shape[0] // 2, across.shape[1]
    n = len(planes)
    rows = planes[0].shape[0]
    factor = head ** (-0.5) * math.log2(math.e)

    def body(*refs):
        qt_ref, gt_ref = refs[0].at[:head, :], refs[0].at[head:, :]
        old_ref, state_ref, score_ref, pgrad_ref = refs[1 + n :]
        keys, values, vt = split(refs[1 : 1 + n], head)
        highs = emit_scores(keys, qt_ref, score_ref, lambda s: s)
        for part, high in zip(parts_of(qt_ref), highs):
            put_state(state_ref, part, *merge(old_ref, part, high, len(keys), vt, score_ref, factor))
        emit_pgrads(values, gt_ref, pgrad_ref)

    kept = ((n * rows, wide), F32)
    state, *kept = call(body, [((head + 8, wide), F32), kept, kept], [], "forward", across, *planes, state)
    return state, kept


def turn(lengths, across, down, planes, state, tokens):
    head, wide = across.shape[0] // 2, across.shape[1]
    n = len(planes)
    rows = n * planes[0].shape[0]
    scale = head ** (-0.5)
    factor = scale * math.log2(math.e)

    def body(*refs):
        lengths_ref, qt_ref, gt_ref = refs[0], refs[1].at[:head, :], refs[1].at[head:, :]
        old_ref, back_ref, att_ref, terms_ref, dscore_ref, score_ref, prob_ref = refs[3 + n :]
        length = own_length(lengths_ref)
        keys, values, vt = split(refs[3 : 3 + n], head)
        highs = emit_scores(keys, qt_ref, score_ref, lambda s: s)
        alive = token_of((1, WIDE), tokens) < length
        for part, high in zip(parts_of(qt_ref), highs):
            top, total, summed = merge(old_ref, part, high, len(keys), vt, score_ref, factor)
            attended = jnp.where(alive, summed / total, 0.0).astype(BF16)
            inner = gt_ref[:, part].astype(F32) * attended.astype(F32)
            back_ref[0:1, part] = top * factor + jnp.log2(total)
            back_ref[1:2, part] = jnp.sum(inner, axis=0, keepdims=True)
            att_ref[:, part] = attended
        emit_dscores(score_ref, lambda i, part: mm(values[i], gt_ref[:, part]), back_ref, prob_ref, dscore_ref, factor)
        emit_terms(prob_ref, dscore_ref, refs[2], terms_ref, scale)

    return call(
        body,
        [((8, wide), F32), ((head, wide), BF16), ((rows, 2 * head), BF16), ((rows, wide), BF16)],
        [pltpu.VMEM((rows, wide), F32), pltpu.VMEM((rows, wide), BF16)],
        "turn",
        lengths, across, down, *planes, state,
    )


def backward(down, back, kept, n):
    wide, head = down.shape[0], down.shape[1] // 2
    rows = kept[0].shape[0] // n
    scale = head ** (-0.5)
    factor = scale * math.log2(math.e)

    def body(*refs):
        down_ref, back_ref, score_ref, pgrad_ref = refs[:4]
        terms, dscores, prob_ref = refs[4 : 4 + n], refs[4 + n : 4 + 2 * n], refs[-1]
        for j in range(n):
            here = slice(j * rows, (j + 1) * rows)
            prob, pgrads = prob_ref.at[here, :], pgrad_ref.at[here, :]
            emit_dscores(
                score_ref.at[here, :],
                lambda i, part: pgrads[i * TILE : (i + 1) * TILE, part],
                back_ref,
                prob,
                dscores[j],
                factor,
            )
            emit_terms(prob, dscores[j], down_ref, terms[j], scale)

    out = call(
        body,
        [((rows, 2 * head), BF16)] * n + [((rows, wide), BF16)] * n,
        [pltpu.VMEM((n * rows, wide), BF16)],
        "backward",
        down, back, *kept,
    )
    return out[:n], out[n:]


def finish(lengths, across, down, back, keys, values, attended, planes, dscores):
    head, wide = across.shape[0] // 2, across.shape[1]
    tokens = keys.shape[0]
    n = len(planes)
    scale = head ** (-0.5)
    factor = scale * math.log2(math.e)

    def body(*refs):
        lengths_ref, across_ref, down_ref, back_ref, k_ref, v_ref, att_ref = refs[:7]
        planes_in, dscores_in = refs[7 : 7 + n], refs[7 + n : -6]
        qt_ref, gt_ref = across_ref.at[:head, :], across_ref.at[head:, :]
        out_ref, dq_ref, dk_ref, dv_ref, prob_ref, dscore_ref = refs[-6:]
        length = own_length(lengths_ref)
        kt = k_ref[...].T
        kts, planes_kt = [x[:, :head].T for x in planes_in], []
        for d in dscores_in:
            group = [kts.pop(0)]
            while sum(k.shape[1] for k in group) < d.shape[0]:
                group.append(kts.pop(0))
            planes_kt.append(jnp.concatenate(group, axis=1))
        for part in parts_of(qt_ref):
            scores = causal(mm(k_ref[...], qt_ref[:, part]), tokens, length)
            pgrad = mm(v_ref[...], gt_ref[:, part])
            prob, dscore = probabilities(scores, pgrad, back_ref, part, factor)
            prob_ref[:, part] = prob
            dscore_ref[:, part] = dscore
            total = mm(kt, dscore)
            for k, d in zip(planes_kt, dscores_in):
                total = total + mm(k, d[:, part])
            out = (total * scale).astype(BF16)
            for i in range(WIDE // tokens):
                h = part.start // tokens + i
                dq_ref[:, h * head : (h + 1) * head] = out[:, i * tokens : (i + 1) * tokens].T
                out_ref[:, h * head : (h + 1) * head] = att_ref[:, h * tokens : (h + 1) * tokens].T
        dk_ref[...] = (mm(dscore_ref[...], down_ref[:, :head]) * scale).astype(BF16)
        dv_ref[...] = mm(prob_ref[...], down_ref[:, head:]).astype(BF16)

    flat = ((tokens, wide // tokens * head), BF16)
    return call(
        body,
        [flat, flat, (keys.shape, BF16), (values.shape, BF16)],
        [pltpu.VMEM((tokens, wide), BF16), pltpu.VMEM((tokens, wide), BF16)],
        "finish",
        lengths, across, down, back, keys, values, attended, *planes, *dscores,
    )


def spread(keys, values, count):
    rows, head = keys.shape

    def body(k_ref, v_ref, out_ref):
        for i in range(count):
            out_ref[i, :, :head] = k_ref[...]
            out_ref[i, :, head:] = v_ref[...]

    return call(body, [((count, rows, 2 * head), BF16)], [], "spread", keys, values, limit=ALL_VMEM_BYTES)[0]


def collect(parts, head):
    def body(in_ref, key_ref, value_ref):
        total = jnp.sum(in_ref[...].astype(F32), axis=0).astype(BF16)
        key_ref[...] = total[:, :head]
        value_ref[...] = total[:, head:]

    shape = ((parts.shape[1], head), BF16)
    return call(body, [shape, shape], [], "collect", parts)


Z_SIZE = 8


def shards(queries, resp_keys, resp_values, prefix_keys, prefix_values, out_grad, lengths, loss_mask):
    group_count = lax.axis_size("grp")
    z_size = Z_SIZE
    y_size = group_count // z_size
    z_groups = [[y * z_size + z for z in range(z_size)] for y in range(y_size)]

    def along_y(x, shift):
        pairs = [(y * z_size + z, (y + shift) % y_size * z_size + z) for y in range(y_size) for z in range(z_size)]
        return lax.ppermute(x, "grp", pairs)

    def along_z(x):
        return lax.all_to_all(x, "grp", 0, 0, axis_index_groups=z_groups, tiled=True)

    own_keys, own_values = resp_keys[0], resp_values[0]
    tokens = own_keys.shape[0]
    rows, head = prefix_keys.shape
    mine = along_z(spread(prefix_keys, prefix_values, z_size)).reshape(z_size * rows, 2 * head)
    across, down, state = start(lengths, queries[0], out_grad[0], loss_mask, own_keys, own_values)
    mine, state = lax.optimization_barrier((mine, state))
    near, other = along_y(mine, 1), along_y(mine, 3)
    state, mine_kept = forward(across, [mine], state)
    near, other, state = lax.optimization_barrier((near, other, state))
    half = mine.shape[0] // 2
    far = [along_y(near[:half], 1), along_y(other[half:], 3)]
    state, kept = forward(across, [near, other], state)
    back, attended, far_terms, far_ds = turn(lengths, across, down, far, state, tokens)
    far_terms = along_y(far_terms, 2)
    (near_terms, other_terms), (near_ds, other_ds) = backward(down, back, kept, 2)
    near_terms, other_terms = along_y(near_terms, 3), along_y(other_terms, 1)
    (mine_terms,), (mine_ds,) = backward(down, back, mine_kept, 1)
    attended, query_grad, key_grad, value_grad = finish(
        lengths, across, down, back, own_keys, own_values, attended,
        [mine, near, other, *far], [mine_ds, near_ds, other_ds, far_ds],
    )
    mine_terms, attended, query_grad, key_grad, value_grad = lax.optimization_barrier(
        (mine_terms, attended, query_grad, key_grad, value_grad)
    )
    part = sum(x.astype(F32) for x in (mine_terms, near_terms, other_terms, far_terms)).astype(BF16)
    key_share, value_share = collect(along_z(part.reshape(z_size, rows, 2 * head)), head)
    return (attended[None], query_grad[None], key_grad[None], value_grad[None], key_share, value_share)


def solution(mesh):
    placed = (
        P(("prompt", "grp"), None, None),
        P(("prompt", "grp"), None, None),
        P(("prompt", "grp"), None, None),
        P(("prompt", "grp"), None),
        P(("prompt", "grp"), None),
        P(("prompt", "grp"), None, None),
        P("prompt"),
        P(("prompt", "grp"), None),
    )
    return jax.shard_map(
        shards,
        mesh=mesh,
        in_specs=placed,
        out_specs=(
            P(("prompt", "grp"), None, None),
            P(("prompt", "grp"), None, None),
            P(("prompt", "grp"), None, None),
            P(("prompt", "grp"), None, None),
            P(("prompt", "grp"), None),
            P(("prompt", "grp"), None),
        ),
        check_vma=False,
    )
```

```python
import math
import jax, jax.numpy as jnp
from jax import lax
from jax.experimental import pallas as pl
from jax.experimental.pallas import tpu as pltpu
from jax.sharding import PartitionSpec as P

F32 = jnp.float32
BF16 = jnp.bfloat16
NEG_BIG = -1e30
TILE = 256
WIDE = 512
VMEM_BYTES = 14 * 2**20
ALL_VMEM_BYTES = 57 * 2**20


def mm(left, right):
    return jnp.dot(left, right, preferred_element_type=F32)


def fold(tile):
    return tile.reshape(tile.shape[0] // 8, 8, tile.shape[1])


def token_of(shape, tokens):
    return lax.rem(lax.broadcasted_iota(jnp.int32, shape, 1), tokens)


def causal(scores, tokens, length):
    key = lax.broadcasted_iota(jnp.int32, scores.shape, 0)
    return jnp.where((key <= token_of(scores.shape, tokens)) & (key < length), scores, NEG_BIG)


def own_length(lengths_ref):
    return lengths_ref[lax.axis_index("grp")]


def parts_of(ref):
    return [slice(i, i + WIDE) for i in range(0, ref.shape[1], WIDE)]


def call(body, out_shape, scratch, name, *args, space=pltpu.VMEM, limit=VMEM_BYTES):
    specs = [pl.BlockSpec(memory_space=pltpu.SMEM if a.ndim == 1 else space) for a in args]
    return pl.pallas_call(
        body,
        in_specs=specs,
        out_specs=[pl.BlockSpec(memory_space=pltpu.VMEM)] * len(out_shape),
        out_shape=[jax.ShapeDtypeStruct(s, d) for s, d in out_shape],
        scratch_shapes=scratch,
        compiler_params=pltpu.CompilerParams(vmem_limit_bytes=limit),
        name=name,
    )(*args)


def put_state(state_ref, part, top, total, summed, length):
    head = state_ref.shape[0] - 8
    state_ref[:head, part] = summed
    state_ref[head : head + 1, part] = top
    state_ref[head + 1 : head + 2, part] = total
    state_ref[head + 2 : head + 3, part] = length


def emit_scores(keys, qt_ref, score_ref, mask):
    highs = []
    for part in parts_of(qt_ref):
        high = None
        for i, k in enumerate(keys):
            scores = mask(mm(k, qt_ref[:, part]))
            score_ref[i * TILE : (i + 1) * TILE, part] = scores
            peak = jnp.max(fold(scores), axis=0)
            high = peak if high is None else jnp.maximum(high, peak)
        highs.append(high)
    return highs


def emit_sums(n, top, vt, score_ref, part, factor, keep=False):
    total, summed = None, None
    for i in range(n):
        weights = jnp.exp2((score_ref[i * TILE : (i + 1) * TILE, part] - top) * factor)
        if keep:
            score_ref[i * TILE : (i + 1) * TILE, part] = weights
        here = jnp.sum(fold(weights), axis=0)
        total = here if total is None else total + here
        here = mm(vt[:, i * TILE : (i + 1) * TILE], weights.astype(BF16))
        summed = here if summed is None else summed + here
    return jnp.sum(total, axis=0, keepdims=True), summed


def start(lengths, queries, grads, mask, keys, values):
    tokens, width = queries.shape
    head = keys.shape[1]
    heads = width // head
    wide = heads * tokens
    factor = head ** (-0.5) * math.log2(math.e)

    def body(
        lengths_ref, q_in, g_in, mask_in, k_in, v_in,
        across_ref, down_ref, state_ref,
        q_ref, g_ref, mask_ref, k_ref, v_ref, score_ref, sems,
    ):
        copies = [
            pltpu.make_async_copy(a, b, sems.at[i])
            for i, (a, b) in enumerate(
                [(q_in, q_ref), (k_in, k_ref), (v_in, v_ref), (mask_in, mask_ref), (g_in, g_ref)]
            )
        ]
        for c in copies:
            c.start()
        length = own_length(lengths_ref)
        qt_ref, gt_ref = across_ref.at[:head, :], across_ref.at[head:, :]
        copies[0].wait()
        for h in range(heads):
            cols, rows = slice(h * head, (h + 1) * head), slice(h * tokens, (h + 1) * tokens)
            q = q_ref[:, cols]
            down_ref[rows, :head] = q
            qt_ref[:, rows] = q.T
        copies[1].wait()
        copies[2].wait()
        highs = emit_scores([k_ref[...]], qt_ref, score_ref, lambda s: causal(s, tokens, length))
        vt = v_ref[...].T
        for part, high in zip(parts_of(qt_ref), highs):
            top = jnp.max(high, axis=0, keepdims=True)
            total, summed = emit_sums(1, top, vt, score_ref, part, factor)
            put_state(state_ref, part, top, total, summed, jnp.full((1, WIDE), length.astype(F32)))
        copies[3].wait()
        copies[4].wait()
        kept = (token_of((1, tokens), tokens) < length) & (mask_ref[...] == 1)
        for h in range(heads):
            cols, rows = slice(h * head, (h + 1) * head), slice(h * tokens, (h + 1) * tokens)
            gt = jnp.where(kept, g_ref[:, cols].T, jnp.zeros((), BF16))
            gt_ref[:, rows] = gt
            down_ref[rows, head:] = gt.T

    args = [queries, grads, mask, keys, values]
    return call(
        body,
        [((2 * head, wide), BF16), ((wide, 2 * head), BF16), ((head + 8, wide), F32)],
        [pltpu.VMEM(x.shape, x.dtype) for x in args]
        + [pltpu.VMEM((tokens, wide), F32), pltpu.SemaphoreType.DMA((5,))],
        "start",
        lengths,
        *args,
        space=pltpu.HBM,
        limit=ALL_VMEM_BYTES,
    )


def emit_pgrads(values, gt_ref, pgrad_ref):
    for part in parts_of(gt_ref):
        for i, v in enumerate(values):
            pgrad_ref[i * TILE : (i + 1) * TILE, part] = mm(v, gt_ref[:, part])


def merge(state_ref, part, high, n, vt, score_ref, factor, keep=False):
    head = state_ref.shape[0] - 8
    before = state_ref[head : head + 1, part]
    top = jnp.maximum(jnp.max(high, axis=0, keepdims=True), before)
    total, summed = emit_sums(n, top, vt, score_ref, part, factor, keep)
    shrink = jnp.exp2((before - top) * factor)
    return top, total + shrink * state_ref[head + 1 : head + 2, part], summed + shrink * state_ref[:head, part]


def probabilities(scores, pgrad, back_ref, part, factor):
    prob = jnp.exp2(scores * factor - back_ref[0:1, part])
    return prob.astype(BF16), (prob * (pgrad - back_ref[1:2, part])).astype(BF16)


def emit_dscores(score_ref, pgrad, back_ref, prob_ref, dscore_ref, factor):
    for part in parts_of(score_ref):
        for i in range(score_ref.shape[0] // TILE):
            here = slice(i * TILE, (i + 1) * TILE)
            prob, dscore = probabilities(score_ref[here, part], pgrad(i, part), back_ref, part, factor)
            prob_ref[here, part] = prob
            dscore_ref[here, part] = dscore


def emit_terms(prob_ref, dscore_ref, down_ref, terms_ref, scale):
    head = down_ref.shape[1] // 2
    for i in range(0, prob_ref.shape[0], TILE):
        here = slice(i, i + TILE)
        terms_ref[here, :head] = (mm(dscore_ref[here, :], down_ref[:, :head]) * scale).astype(BF16)
        terms_ref[here, head:] = mm(prob_ref[here, :], down_ref[:, head:]).astype(BF16)


def split(planes_in, head):
    keys = [x[i : i + TILE, :head] for x in planes_in for i in range(0, x.shape[0], TILE)]
    values = [x[i : i + TILE, head:] for x in planes_in for i in range(0, x.shape[0], TILE)]
    vt = jnp.concatenate([x[:, head:].T for x in planes_in], axis=1)
    return keys, values, vt


def forward(across, planes, state):
    head, wide = across.shape[0] // 2, across.shape[1]
    n = len(planes)
    rows = planes[0].shape[0]
    factor = head ** (-0.5) * math.log2(math.e)

    def body(*refs):
        qt_ref, gt_ref = refs[0].at[:head, :], refs[0].at[head:, :]
        old_ref, state_ref, score_ref, pgrad_ref = refs[1 + n :]
        keys, values, vt = split(refs[1 : 1 + n], head)
        highs = emit_scores(keys, qt_ref, score_ref, lambda s: s)
        for part, high in zip(parts_of(qt_ref), highs):
            merged = merge(old_ref, part, high, len(keys), vt, score_ref, factor)
            put_state(state_ref, part, *merged, old_ref[head + 2 : head + 3, part])
        emit_pgrads(values, gt_ref, pgrad_ref)

    kept = ((n * rows, wide), F32)
    state, *kept = call(body, [((head + 8, wide), F32), kept, kept], [], "forward", across, *planes, state)
    return state, kept


def turn(across, down, planes, state, tokens):
    head, wide = across.shape[0] // 2, across.shape[1]
    n = len(planes)
    rows = n * planes[0].shape[0]
    scale = head ** (-0.5)
    factor = scale * math.log2(math.e)

    def body(*refs):
        qt_ref, gt_ref, down_ref = refs[0].at[:head, :], refs[0].at[head:, :], refs[1]
        old_ref, back_ref, att_ref, terms_ref, dscore_ref, score_ref, prob_ref = refs[2 + n :]
        keys, values, vt = split(refs[2 : 2 + n], head)
        highs = emit_scores(keys, qt_ref, score_ref, lambda s: s)
        for part, high in zip(parts_of(qt_ref), highs):
            top, total, summed = merge(old_ref, part, high, len(keys), vt, score_ref, factor, keep=True)
            length = old_ref[head + 2 : head + 3, part]
            alive = token_of((1, WIDE), tokens) < length.astype(jnp.int32)
            share = 1.0 / total
            attended = jnp.where(alive, summed * share, 0.0).astype(BF16)
            inner = gt_ref[:, part].astype(F32) * attended.astype(F32)
            inner = jnp.sum(inner, axis=0, keepdims=True)
            back_ref[0:1, part] = top * factor + jnp.log2(total)
            back_ref[1:2, part] = inner
            back_ref[2:3, part] = length
            att_ref[:, part] = attended
            for i, v in enumerate(values):
                here = slice(i * TILE, (i + 1) * TILE)
                prob = score_ref[here, part] * share
                prob_ref[here, part] = prob.astype(BF16)
                dscore_ref[here, part] = (prob * (mm(v, gt_ref[:, part]) - inner)).astype(BF16)
        emit_terms(prob_ref, dscore_ref, down_ref, terms_ref, scale)

    return call(
        body,
        [((8, wide), F32), ((head, wide), BF16), ((rows, 2 * head), BF16), ((rows, wide), BF16)],
        [pltpu.VMEM((rows, wide), F32), pltpu.VMEM((rows, wide), BF16)],
        "turn",
        across, down, *planes, state,
    )


def backward(down, back, kept, n):
    wide, head = down.shape[0], down.shape[1] // 2
    rows = kept[0].shape[0] // n
    scale = head ** (-0.5)
    factor = scale * math.log2(math.e)

    def body(*refs):
        down_ref, back_ref, score_ref, pgrad_ref = refs[:4]
        terms, dscores, prob_ref = refs[4 : 4 + n], refs[4 + n : 4 + 2 * n], refs[-1]
        for j in range(n):
            here = slice(j * rows, (j + 1) * rows)
            prob, pgrads = prob_ref.at[here, :], pgrad_ref.at[here, :]
            emit_dscores(
                score_ref.at[here, :],
                lambda i, part: pgrads[i * TILE : (i + 1) * TILE, part],
                back_ref,
                prob,
                dscores[j],
                factor,
            )
            emit_terms(prob, dscores[j], down_ref, terms[j], scale)

    out = call(
        body,
        [((rows, 2 * head), BF16)] * n + [((rows, wide), BF16)] * n,
        [pltpu.VMEM((n * rows, wide), BF16)],
        "backward",
        down, back, *kept,
    )
    return out[:n], out[n:]


def finish(across, down, back, keys, values, attended, planes, dscores):
    head, wide = across.shape[0] // 2, across.shape[1]
    tokens = keys.shape[0]
    n = len(planes)
    scale = head ** (-0.5)
    factor = scale * math.log2(math.e)

    def body(*refs):
        across_ref, down_ref, back_ref, k_ref, v_ref, att_ref = refs[:6]
        planes_in, dscores_in = refs[6 : 6 + n], refs[6 + n : -6]
        qt_ref, gt_ref = across_ref.at[:head, :], across_ref.at[head:, :]
        out_ref, dq_ref, dk_ref, dv_ref, prob_ref, dscore_ref = refs[-6:]
        kt = k_ref[...].T
        kts, planes_kt = [x[:, :head].T for x in planes_in], []
        for d in dscores_in:
            group = [kts.pop(0)]
            while sum(k.shape[1] for k in group) < d.shape[0]:
                group.append(kts.pop(0))
            planes_kt.append(jnp.concatenate(group, axis=1))
        for part in parts_of(qt_ref):
            length = back_ref[2:3, part].astype(jnp.int32)
            scores = causal(mm(k_ref[...], qt_ref[:, part]), tokens, length)
            pgrad = mm(v_ref[...], gt_ref[:, part])
            prob, dscore = probabilities(scores, pgrad, back_ref, part, factor)
            prob_ref[:, part] = prob
            dscore_ref[:, part] = dscore
            total = mm(kt, dscore)
            for k, d in zip(planes_kt, dscores_in):
                total = total + mm(k, d[:, part])
            out = (total * scale).astype(BF16)
            for i in range(WIDE // tokens):
                h = part.start // tokens + i
                dq_ref[:, h * head : (h + 1) * head] = out[:, i * tokens : (i + 1) * tokens].T
                out_ref[:, h * head : (h + 1) * head] = att_ref[:, h * tokens : (h + 1) * tokens].T
        dk_ref[...] = (mm(dscore_ref[...], down_ref[:, :head]) * scale).astype(BF16)
        dv_ref[...] = mm(prob_ref[...], down_ref[:, head:]).astype(BF16)

    flat = ((tokens, wide // tokens * head), BF16)
    return call(
        body,
        [flat, flat, (keys.shape, BF16), (values.shape, BF16)],
        [pltpu.VMEM((tokens, wide), BF16), pltpu.VMEM((tokens, wide), BF16)],
        "finish",
        across, down, back, keys, values, attended, *planes, *dscores,
    )


def spread(keys, values, count):
    rows, head = keys.shape

    def body(k_ref, v_ref, out_ref):
        for i in range(count):
            out_ref[i, :, :head] = k_ref[...]
            out_ref[i, :, head:] = v_ref[...]

    return call(body, [((count, rows, 2 * head), BF16)], [], "spread", keys, values, limit=ALL_VMEM_BYTES)[0]


def collect(parts, head):
    def body(in_ref, key_ref, value_ref):
        total = jnp.sum(in_ref[...].astype(F32), axis=0).astype(BF16)
        key_ref[...] = total[:, :head]
        value_ref[...] = total[:, head:]

    shape = ((parts.shape[1], head), BF16)
    return call(body, [shape, shape], [], "collect", parts)


Z_SIZE = 8


def shards(queries, resp_keys, resp_values, prefix_keys, prefix_values, out_grad, lengths, loss_mask):
    group_count = lax.axis_size("grp")
    z_size = Z_SIZE
    y_size = group_count // z_size
    z_groups = [[y * z_size + z for z in range(z_size)] for y in range(y_size)]

    def along_y(x, shift):
        pairs = [(y * z_size + z, (y + shift) % y_size * z_size + z) for y in range(y_size) for z in range(z_size)]
        return lax.ppermute(x, "grp", pairs)

    def along_z(x):
        return lax.all_to_all(x, "grp", 0, 0, axis_index_groups=z_groups, tiled=True)

    own_keys, own_values = resp_keys[0], resp_values[0]
    tokens = own_keys.shape[0]
    rows, head = prefix_keys.shape
    mine = along_z(spread(prefix_keys, prefix_values, z_size)).reshape(z_size * rows, 2 * head)
    across, down, state = start(lengths, queries[0], out_grad[0], loss_mask, own_keys, own_values)
    mine, state = lax.optimization_barrier((mine, state))
    near, other = along_y(mine, 1), along_y(mine, 3)
    state, mine_kept = forward(across, [mine], state)
    near, other, state = lax.optimization_barrier((near, other, state))
    half = mine.shape[0] // 2
    far = [along_y(near[:half], 1), along_y(other[half:], 3)]
    state, kept = forward(across, [near, other], state)
    back, attended, far_terms, far_ds = turn(across, down, far, state, tokens)
    far_terms = along_y(far_terms, 2)
    (near_terms, other_terms), (near_ds, other_ds) = backward(down, back, kept, 2)
    near_terms, other_terms = along_y(near_terms, 3), along_y(other_terms, 1)
    (mine_terms,), (mine_ds,) = backward(down, back, mine_kept, 1)
    attended, query_grad, key_grad, value_grad = finish(
        across, down, back, own_keys, own_values, attended,
        [mine, near, other, *far], [mine_ds, near_ds, other_ds, far_ds],
    )
    mine_terms, attended, query_grad, key_grad, value_grad = lax.optimization_barrier(
        (mine_terms, attended, query_grad, key_grad, value_grad)
    )
    part = sum(x.astype(F32) for x in (mine_terms, near_terms, other_terms, far_terms)).astype(BF16)
    key_share, value_share = collect(along_z(part.reshape(z_size, rows, 2 * head)), head)
    return (attended[None], query_grad[None], key_grad[None], value_grad[None], key_share, value_share)


def solution(mesh):
    placed = (
        P(("prompt", "grp"), None, None),
        P(("prompt", "grp"), None, None),
        P(("prompt", "grp"), None, None),
        P(("prompt", "grp"), None),
        P(("prompt", "grp"), None),
        P(("prompt", "grp"), None, None),
        P("prompt"),
        P(("prompt", "grp"), None),
    )
    return jax.shard_map(
        shards,
        mesh=mesh,
        in_specs=placed,
        out_specs=(
            P(("prompt", "grp"), None, None),
            P(("prompt", "grp"), None, None),
            P(("prompt", "grp"), None, None),
            P(("prompt", "grp"), None, None),
            P(("prompt", "grp"), None),
            P(("prompt", "grp"), None),
        ),
        check_vma=False,
    )
```

```python
import math
import jax, jax.numpy as jnp
from jax import lax
from jax.experimental import pallas as pl
from jax.experimental.pallas import tpu as pltpu
from jax.sharding import PartitionSpec as P

F32 = jnp.float32
BF16 = jnp.bfloat16
NEG_BIG = -1e30
TILE = 256
WIDE = 512
VMEM_BYTES = 14 * 2**20
ALL_VMEM_BYTES = 57 * 2**20


def mm(left, right):
    return jnp.dot(left, right, preferred_element_type=F32)


def fold(tile):
    return tile.reshape(tile.shape[0] // 8, 8, tile.shape[1])


def token_of(shape, tokens):
    return lax.rem(lax.broadcasted_iota(jnp.int32, shape, 1), tokens)


def causal(scores, tokens, length):
    key = lax.broadcasted_iota(jnp.int32, scores.shape, 0)
    return jnp.where((key <= token_of(scores.shape, tokens)) & (key < length), scores, NEG_BIG)


def own_length(lengths_ref):
    return lengths_ref[lax.axis_index("grp")]


def parts_of(ref):
    return [slice(i, i + WIDE) for i in range(0, ref.shape[1], WIDE)]


def call(body, out_shape, scratch, name, *args, space=pltpu.VMEM, limit=VMEM_BYTES):
    specs = [pl.BlockSpec(memory_space=pltpu.SMEM if a.ndim == 1 else space) for a in args]
    return pl.pallas_call(
        body,
        in_specs=specs,
        out_specs=[pl.BlockSpec(memory_space=pltpu.VMEM)] * len(out_shape),
        out_shape=[jax.ShapeDtypeStruct(s, d) for s, d in out_shape],
        scratch_shapes=scratch,
        compiler_params=pltpu.CompilerParams(vmem_limit_bytes=limit),
        name=name,
    )(*args)


def put_state(state_ref, part, top, total, summed, length):
    head = state_ref.shape[0] - 8
    state_ref[:head, part] = summed
    state_ref[head : head + 1, part] = top
    state_ref[head + 1 : head + 2, part] = total
    state_ref[head + 2 : head + 3, part] = length


def emit_scores(keys, qt_ref, score_ref, mask):
    highs = []
    for part in parts_of(qt_ref):
        high = None
        for i, k in enumerate(keys):
            scores = mask(mm(k, qt_ref[:, part]))
            score_ref[i * TILE : (i + 1) * TILE, part] = scores
            peak = jnp.max(fold(scores), axis=0)
            high = peak if high is None else jnp.maximum(high, peak)
        highs.append(high)
    return highs


def emit_sums(n, top, vt, score_ref, part, factor, keep=False):
    total, summed = None, None
    for i in range(n):
        weights = jnp.exp2((score_ref[i * TILE : (i + 1) * TILE, part] - top) * factor)
        if keep:
            score_ref[i * TILE : (i + 1) * TILE, part] = weights
        here = jnp.sum(fold(weights), axis=0)
        total = here if total is None else total + here
        here = mm(vt[:, i * TILE : (i + 1) * TILE], weights.astype(BF16))
        summed = here if summed is None else summed + here
    return jnp.sum(total, axis=0, keepdims=True), summed


def start(lengths, queries, grads, mask, keys, values):
    tokens, width = queries.shape
    head = keys.shape[1]
    heads = width // head
    wide = heads * tokens
    factor = head ** (-0.5) * math.log2(math.e)

    def body(
        lengths_ref, q_in, g_in, mask_in, k_in, v_in,
        across_ref, down_ref, state_ref,
        q_ref, g_ref, mask_ref, k_ref, v_ref, score_ref, sems,
    ):
        copies = [
            pltpu.make_async_copy(a, b, sems.at[i])
            for i, (a, b) in enumerate(
                [(q_in, q_ref), (k_in, k_ref), (v_in, v_ref), (mask_in, mask_ref), (g_in, g_ref)]
            )
        ]
        for c in copies:
            c.start()
        length = own_length(lengths_ref)
        qt_ref, gt_ref = across_ref.at[:head, :], across_ref.at[head:, :]
        copies[0].wait()
        for h in range(heads):
            cols, rows = slice(h * head, (h + 1) * head), slice(h * tokens, (h + 1) * tokens)
            q = q_ref[:, cols]
            down_ref[rows, :head] = q
            qt_ref[:, rows] = q.T
        copies[1].wait()
        copies[2].wait()
        highs = emit_scores([k_ref[...]], qt_ref, score_ref, lambda s: causal(s, tokens, length))
        vt = v_ref[...].T
        for part, high in zip(parts_of(qt_ref), highs):
            top = jnp.max(high, axis=0, keepdims=True)
            total, summed = emit_sums(1, top, vt, score_ref, part, factor)
            put_state(state_ref, part, top, total, summed, jnp.full((1, WIDE), length.astype(F32)))
        copies[3].wait()
        copies[4].wait()
        kept = (token_of((1, tokens), tokens) < length) & (mask_ref[...] == 1)
        for h in range(heads):
            cols, rows = slice(h * head, (h + 1) * head), slice(h * tokens, (h + 1) * tokens)
            gt = jnp.where(kept, g_ref[:, cols].T, jnp.zeros((), BF16))
            gt_ref[:, rows] = gt
            down_ref[rows, head:] = gt.T

    args = [queries, grads, mask, keys, values]
    return call(
        body,
        [((2 * head, wide), BF16), ((wide, 2 * head), BF16), ((head + 8, wide), F32)],
        [pltpu.VMEM(x.shape, x.dtype) for x in args]
        + [pltpu.VMEM((tokens, wide), F32), pltpu.SemaphoreType.DMA((5,))],
        "start",
        lengths,
        *args,
        space=pltpu.HBM,
        limit=ALL_VMEM_BYTES,
    )


def emit_pgrads(values, gt_ref, pgrad_ref):
    for part in parts_of(gt_ref):
        for i, v in enumerate(values):
            pgrad_ref[i * TILE : (i + 1) * TILE, part] = mm(v, gt_ref[:, part])


def merge(state_ref, part, high, n, vt, score_ref, factor, keep=False):
    head = state_ref.shape[0] - 8
    before = state_ref[head : head + 1, part]
    top = jnp.maximum(jnp.max(high, axis=0, keepdims=True), before)
    total, summed = emit_sums(n, top, vt, score_ref, part, factor, keep)
    shrink = jnp.exp2((before - top) * factor)
    return top, total + shrink * state_ref[head + 1 : head + 2, part], summed + shrink * state_ref[:head, part]


def probabilities(scores, pgrad, back_ref, part, factor):
    prob = jnp.exp2(scores * factor - back_ref[0:1, part])
    return prob.astype(BF16), (prob * (pgrad - back_ref[1:2, part])).astype(BF16)


def emit_dscores(score_ref, pgrad, back_ref, prob_ref, dscore_ref, factor):
    for part in parts_of(score_ref):
        for i in range(score_ref.shape[0] // TILE):
            here = slice(i * TILE, (i + 1) * TILE)
            prob, dscore = probabilities(score_ref[here, part], pgrad(i, part), back_ref, part, factor)
            prob_ref[here, part] = prob
            dscore_ref[here, part] = dscore


def emit_terms(prob_ref, dscore_ref, down_ref, terms_ref, scale):
    head = down_ref.shape[1] // 2
    for i in range(0, prob_ref.shape[0], TILE):
        here = slice(i, i + TILE)
        terms_ref[here, :head] = (mm(dscore_ref[here, :], down_ref[:, :head]) * scale).astype(BF16)
        terms_ref[here, head:] = mm(prob_ref[here, :], down_ref[:, head:]).astype(BF16)


def split(planes_in, head):
    keys = [x[i : i + TILE, :head] for x in planes_in for i in range(0, x.shape[0], TILE)]
    values = [x[i : i + TILE, head:] for x in planes_in for i in range(0, x.shape[0], TILE)]
    vt = jnp.concatenate([x[:, head:].T for x in planes_in], axis=1)
    return keys, values, vt


def forward(across, planes, state):
    head, wide = across.shape[0] // 2, across.shape[1]
    n = len(planes)
    rows = planes[0].shape[0]
    factor = head ** (-0.5) * math.log2(math.e)

    def body(*refs):
        qt_ref, gt_ref = refs[0].at[:head, :], refs[0].at[head:, :]
        old_ref, state_ref, score_ref, pgrad_ref = refs[1 + n :]
        keys, values, vt = split(refs[1 : 1 + n], head)
        highs = emit_scores(keys, qt_ref, score_ref, lambda s: s)
        for part, high in zip(parts_of(qt_ref), highs):
            merged = merge(old_ref, part, high, len(keys), vt, score_ref, factor)
            put_state(state_ref, part, *merged, old_ref[head + 2 : head + 3, part])
        emit_pgrads(values, gt_ref, pgrad_ref)

    kept = ((n * rows, wide), F32)
    state, *kept = call(body, [((head + 8, wide), F32), kept, kept], [], "forward", across, *planes, state)
    return state, kept


def turn(across, down, planes, state, tokens):
    head, wide = across.shape[0] // 2, across.shape[1]
    n = len(planes)
    rows = n * planes[0].shape[0]
    scale = head ** (-0.5)
    factor = scale * math.log2(math.e)

    def body(*refs):
        qt_ref, gt_ref, down_ref = refs[0].at[:head, :], refs[0].at[head:, :], refs[1]
        old_ref, back_ref, att_ref, terms_ref, dscore_ref, score_ref, prob_ref = refs[2 + n :]
        keys, values, vt = split(refs[2 : 2 + n], head)
        highs = emit_scores(keys, qt_ref, score_ref, lambda s: s)
        for part, high in zip(parts_of(qt_ref), highs):
            top, total, summed = merge(old_ref, part, high, len(keys), vt, score_ref, factor, keep=True)
            length = old_ref[head + 2 : head + 3, part]
            alive = token_of((1, WIDE), tokens) < length.astype(jnp.int32)
            share = 1.0 / total
            attended = jnp.where(alive, summed * share, 0.0).astype(BF16)
            inner = gt_ref[:, part].astype(F32) * attended.astype(F32)
            inner = jnp.sum(inner, axis=0, keepdims=True)
            back_ref[0:1, part] = top * factor + jnp.log2(total)
            back_ref[1:2, part] = inner
            back_ref[2:3, part] = length
            att_ref[:, part] = attended
            for i, v in enumerate(values):
                here = slice(i * TILE, (i + 1) * TILE)
                prob = score_ref[here, part] * share
                prob_ref[here, part] = prob.astype(BF16)
                dscore_ref[here, part] = (prob * (mm(v, gt_ref[:, part]) - inner)).astype(BF16)
        emit_terms(prob_ref, dscore_ref, down_ref, terms_ref, scale)

    return call(
        body,
        [((8, wide), F32), ((head, wide), BF16), ((rows, 2 * head), BF16), ((rows, wide), BF16)],
        [pltpu.VMEM((rows, wide), F32), pltpu.VMEM((rows, wide), BF16)],
        "turn",
        across, down, *planes, state,
    )


def backward(down, back, kept, n):
    wide, head = down.shape[0], down.shape[1] // 2
    rows = kept[0].shape[0] // n
    scale = head ** (-0.5)
    factor = scale * math.log2(math.e)

    def body(*refs):
        down_ref, back_ref, score_ref, pgrad_ref = refs[:4]
        terms, dscores, prob_ref = refs[4 : 4 + n], refs[4 + n : 4 + 2 * n], refs[-1]
        for j in range(n):
            here = slice(j * rows, (j + 1) * rows)
            prob, pgrads = prob_ref.at[here, :], pgrad_ref.at[here, :]
            emit_dscores(
                score_ref.at[here, :],
                lambda i, part: pgrads[i * TILE : (i + 1) * TILE, part],
                back_ref,
                prob,
                dscores[j],
                factor,
            )
            emit_terms(prob, dscores[j], down_ref, terms[j], scale)

    out = call(
        body,
        [((rows, 2 * head), BF16)] * n + [((rows, wide), BF16)] * n,
        [pltpu.VMEM((n * rows, wide), BF16)],
        "backward",
        down, back, *kept,
    )
    return out[:n], out[n:]


def finish(across, down, back, keys, values, attended, planes, dscores):
    head, wide = across.shape[0] // 2, across.shape[1]
    tokens = keys.shape[0]
    n = len(planes)
    scale = head ** (-0.5)
    factor = scale * math.log2(math.e)

    def body(*refs):
        across_ref, down_ref, back_ref, k_ref, v_ref, att_ref = refs[:6]
        planes_in, dscores_in = refs[6 : 6 + n], refs[6 + n : -6]
        qt_ref, gt_ref = across_ref.at[:head, :], across_ref.at[head:, :]
        out_ref, dq_ref, dk_ref, dv_ref, prob_ref, dscore_ref = refs[-6:]
        kt = k_ref[...].T
        kts, planes_kt = [x[:, :head].T for x in planes_in], []
        for d in dscores_in:
            group = [kts.pop(0)]
            while sum(k.shape[1] for k in group) < d.shape[0]:
                group.append(kts.pop(0))
            planes_kt.append(jnp.concatenate(group, axis=1))
        for part in parts_of(qt_ref):
            length = back_ref[2:3, part].astype(jnp.int32)
            scores = causal(mm(k_ref[...], qt_ref[:, part]), tokens, length)
            pgrad = mm(v_ref[...], gt_ref[:, part])
            prob, dscore = probabilities(scores, pgrad, back_ref, part, factor)
            prob_ref[:, part] = prob
            dscore_ref[:, part] = dscore
            total = mm(kt, dscore)
            for k, d in zip(planes_kt, dscores_in):
                total = total + mm(k, d[:, part])
            out = (total * scale).astype(BF16)
            for i in range(WIDE // tokens):
                h = part.start // tokens + i
                dq_ref[:, h * head : (h + 1) * head] = out[:, i * tokens : (i + 1) * tokens].T
                out_ref[:, h * head : (h + 1) * head] = att_ref[:, h * tokens : (h + 1) * tokens].T
        dk_ref[...] = (mm(dscore_ref[...], down_ref[:, :head]) * scale).astype(BF16)
        dv_ref[...] = mm(prob_ref[...], down_ref[:, head:]).astype(BF16)

    flat = ((tokens, wide // tokens * head), BF16)
    return call(
        body,
        [flat, flat, (keys.shape, BF16), (values.shape, BF16)],
        [pltpu.VMEM((tokens, wide), BF16), pltpu.VMEM((tokens, wide), BF16)],
        "finish",
        across, down, back, keys, values, attended, *planes, *dscores,
    )


def spread(keys, values, count):
    rows, head = keys.shape

    def body(k_ref, v_ref, out_ref):
        for i in range(count):
            out_ref[i, :, :head] = k_ref[...]
            out_ref[i, :, head:] = v_ref[...]

    return call(body, [((count, rows, 2 * head), BF16)], [], "spread", keys, values, limit=ALL_VMEM_BYTES)[0]


def collect(parts, head):
    def body(in_ref, key_ref, value_ref):
        total = jnp.sum(in_ref[...].astype(F32), axis=0).astype(BF16)
        key_ref[...] = total[:, :head]
        value_ref[...] = total[:, head:]

    shape = ((parts.shape[1], head), BF16)
    return call(body, [shape, shape], [], "collect", parts)


Z_SIZE = 8


def shards(queries, resp_keys, resp_values, prefix_keys, prefix_values, out_grad, lengths, loss_mask):
    group_count = lax.axis_size("grp")
    z_size = Z_SIZE
    y_size = group_count // z_size
    z_groups = [[y * z_size + z for z in range(z_size)] for y in range(y_size)]

    def along_y(x, shift):
        pairs = [(y * z_size + z, (y + shift) % y_size * z_size + z) for y in range(y_size) for z in range(z_size)]
        return lax.ppermute(x, "grp", pairs)

    def along_z(x):
        return lax.all_to_all(x, "grp", 0, 0, axis_index_groups=z_groups, tiled=True)

    own_keys, own_values = resp_keys[0], resp_values[0]
    tokens = own_keys.shape[0]
    rows, head = prefix_keys.shape
    mine = along_z(spread(prefix_keys, prefix_values, z_size)).reshape(z_size * rows, 2 * head)
    across, down, state = start(lengths, queries[0], out_grad[0], loss_mask, own_keys, own_values)
    mine, state = lax.optimization_barrier((mine, state))
    near, other = along_y(mine, 1), along_y(mine, 3)
    state, mine_kept = forward(across, [mine], state)
    half = mine.shape[0] // 2
    near, state = lax.optimization_barrier((near, state))
    far = [along_y(near[:half], 1)]
    other, state = lax.optimization_barrier((other, state))
    far.append(along_y(other[half:], 3))
    state, kept = forward(across, [near, other], state)
    back, attended, far_terms, far_ds = turn(across, down, far, state, tokens)
    far_terms = along_y(far_terms, 2)
    (near_terms, other_terms), (near_ds, other_ds) = backward(down, back, kept, 2)
    near_terms, other_terms = along_y(near_terms, 3), along_y(other_terms, 1)
    (mine_terms,), (mine_ds,) = backward(down, back, mine_kept, 1)
    attended, query_grad, key_grad, value_grad = finish(
        across, down, back, own_keys, own_values, attended,
        [mine, near, other, *far], [mine_ds, near_ds, other_ds, far_ds],
    )
    mine_terms, attended, query_grad, key_grad, value_grad = lax.optimization_barrier(
        (mine_terms, attended, query_grad, key_grad, value_grad)
    )
    part = sum(x.astype(F32) for x in (mine_terms, near_terms, other_terms, far_terms)).astype(BF16)
    key_share, value_share = collect(along_z(part.reshape(z_size, rows, 2 * head)), head)
    return (attended[None], query_grad[None], key_grad[None], value_grad[None], key_share, value_share)


def solution(mesh):
    placed = (
        P(("prompt", "grp"), None, None),
        P(("prompt", "grp"), None, None),
        P(("prompt", "grp"), None, None),
        P(("prompt", "grp"), None),
        P(("prompt", "grp"), None),
        P(("prompt", "grp"), None, None),
        P("prompt"),
        P(("prompt", "grp"), None),
    )
    return jax.shard_map(
        shards,
        mesh=mesh,
        in_specs=placed,
        out_specs=(
            P(("prompt", "grp"), None, None),
            P(("prompt", "grp"), None, None),
            P(("prompt", "grp"), None, None),
            P(("prompt", "grp"), None, None),
            P(("prompt", "grp"), None),
            P(("prompt", "grp"), None),
        ),
        check_vma=False,
    )
```

```python
import math
import jax, jax.numpy as jnp
from jax import lax
from jax.experimental import pallas as pl
from jax.experimental.pallas import tpu as pltpu
from jax.sharding import PartitionSpec as P

F32 = jnp.float32
BF16 = jnp.bfloat16
NEG_BIG = -1e30
TILE = 256
WIDE = 512
VMEM_BYTES = 14 * 2**20
ALL_VMEM_BYTES = 57 * 2**20


def mm(left, right):
    return jnp.dot(left, right, preferred_element_type=F32)


def fold(tile):
    return tile.reshape(tile.shape[0] // 8, 8, tile.shape[1])


def token_of(shape, tokens):
    return lax.rem(lax.broadcasted_iota(jnp.int32, shape, 1), tokens)


def causal(scores, tokens, length):
    key = lax.broadcasted_iota(jnp.int32, scores.shape, 0)
    return jnp.where((key <= token_of(scores.shape, tokens)) & (key < length), scores, NEG_BIG)


def own_length(lengths_ref):
    return lengths_ref[lax.axis_index("grp")]


def parts_of(ref):
    return [slice(i, i + WIDE) for i in range(0, ref.shape[1], WIDE)]


def call(body, out_shape, scratch, name, *args, space=pltpu.VMEM, limit=VMEM_BYTES):
    specs = [pl.BlockSpec(memory_space=pltpu.SMEM if a.ndim == 1 else space) for a in args]
    return pl.pallas_call(
        body,
        in_specs=specs,
        out_specs=[pl.BlockSpec(memory_space=pltpu.VMEM)] * len(out_shape),
        out_shape=[jax.ShapeDtypeStruct(s, d) for s, d in out_shape],
        scratch_shapes=scratch,
        compiler_params=pltpu.CompilerParams(vmem_limit_bytes=limit),
        name=name,
    )(*args)


def put_state(state_ref, part, top, total, summed, length):
    head = state_ref.shape[0] - 8
    state_ref[:head, part] = summed
    state_ref[head : head + 1, part] = top
    state_ref[head + 1 : head + 2, part] = total
    state_ref[head + 2 : head + 3, part] = length


def emit_scores(keys, qt_ref, score_ref, mask):
    highs = []
    for part in parts_of(qt_ref):
        high = None
        for i, k in enumerate(keys):
            scores = mask(mm(k, qt_ref[:, part]))
            score_ref[i * TILE : (i + 1) * TILE, part] = scores
            peak = jnp.max(fold(scores), axis=0)
            high = peak if high is None else jnp.maximum(high, peak)
        highs.append(high)
    return highs


def emit_sums(n, top, vt, score_ref, part, factor, keep=False):
    total, summed = None, None
    for i in range(n):
        weights = jnp.exp2((score_ref[i * TILE : (i + 1) * TILE, part] - top) * factor)
        if keep:
            score_ref[i * TILE : (i + 1) * TILE, part] = weights
        here = jnp.sum(fold(weights), axis=0)
        total = here if total is None else total + here
        here = mm(vt[:, i * TILE : (i + 1) * TILE], weights.astype(BF16))
        summed = here if summed is None else summed + here
    return jnp.sum(total, axis=0, keepdims=True), summed


def start(lengths, queries, grads, mask, keys, values):
    tokens, width = queries.shape
    head = keys.shape[1]
    heads = width // head
    wide = heads * tokens
    factor = head ** (-0.5) * math.log2(math.e)

    def body(
        lengths_ref, q_in, g_in, mask_in, k_in, v_in,
        across_ref, down_ref, state_ref,
        q_ref, g_ref, mask_ref, k_ref, v_ref, score_ref, sems,
    ):
        copies = [
            pltpu.make_async_copy(a, b, sems.at[i])
            for i, (a, b) in enumerate(
                [(q_in, q_ref), (k_in, k_ref), (v_in, v_ref), (mask_in, mask_ref), (g_in, g_ref)]
            )
        ]
        for c in copies:
            c.start()
        length = own_length(lengths_ref)
        qt_ref, gt_ref = across_ref.at[:head, :], across_ref.at[head:, :]
        copies[0].wait()
        for h in range(heads):
            cols, rows = slice(h * head, (h + 1) * head), slice(h * tokens, (h + 1) * tokens)
            q = q_ref[:, cols]
            down_ref[rows, :head] = q
            qt_ref[:, rows] = q.T
        copies[1].wait()
        copies[2].wait()
        highs = emit_scores([k_ref[...]], qt_ref, score_ref, lambda s: causal(s, tokens, length))
        vt = v_ref[...].T
        for part, high in zip(parts_of(qt_ref), highs):
            top = jnp.max(high, axis=0, keepdims=True)
            total, summed = emit_sums(1, top, vt, score_ref, part, factor)
            put_state(state_ref, part, top, total, summed, jnp.full((1, WIDE), length.astype(F32)))
        copies[3].wait()
        copies[4].wait()
        kept = (token_of((1, tokens), tokens) < length) & (mask_ref[...] == 1)
        for h in range(heads):
            cols, rows = slice(h * head, (h + 1) * head), slice(h * tokens, (h + 1) * tokens)
            gt = jnp.where(kept, g_ref[:, cols].T, jnp.zeros((), BF16))
            gt_ref[:, rows] = gt
            down_ref[rows, head:] = gt.T

    args = [queries, grads, mask, keys, values]
    return call(
        body,
        [((2 * head, wide), BF16), ((wide, 2 * head), BF16), ((head + 8, wide), F32)],
        [pltpu.VMEM(x.shape, x.dtype) for x in args]
        + [pltpu.VMEM((tokens, wide), F32), pltpu.SemaphoreType.DMA((5,))],
        "start",
        lengths,
        *args,
        space=pltpu.HBM,
        limit=ALL_VMEM_BYTES,
    )


def emit_pgrads(values, gt_ref, pgrad_ref):
    for part in parts_of(gt_ref):
        for i, v in enumerate(values):
            pgrad_ref[i * TILE : (i + 1) * TILE, part] = mm(v, gt_ref[:, part])


def merge(state_ref, part, high, n, vt, score_ref, factor, keep=False):
    head = state_ref.shape[0] - 8
    before = state_ref[head : head + 1, part]
    top = jnp.maximum(jnp.max(high, axis=0, keepdims=True), before)
    total, summed = emit_sums(n, top, vt, score_ref, part, factor, keep)
    shrink = jnp.exp2((before - top) * factor)
    return top, total + shrink * state_ref[head + 1 : head + 2, part], summed + shrink * state_ref[:head, part]


def probabilities(scores, pgrad, back_ref, part, factor):
    prob = jnp.exp2(scores * factor - back_ref[0:1, part])
    return prob.astype(BF16), (prob * (pgrad - back_ref[1:2, part])).astype(BF16)


def emit_dscores(score_ref, pgrad, back_ref, prob_ref, dscore_ref, factor):
    for part in parts_of(score_ref):
        for i in range(score_ref.shape[0] // TILE):
            here = slice(i * TILE, (i + 1) * TILE)
            prob, dscore = probabilities(score_ref[here, part], pgrad(i, part), back_ref, part, factor)
            prob_ref[here, part] = prob
            dscore_ref[here, part] = dscore


def emit_terms(prob_ref, dscore_ref, down_ref, terms_ref, scale):
    head = down_ref.shape[1] // 2
    for i in range(0, prob_ref.shape[0], TILE):
        here = slice(i, i + TILE)
        terms_ref[here, :head] = (mm(dscore_ref[here, :], down_ref[:, :head]) * scale).astype(BF16)
        terms_ref[here, head:] = mm(prob_ref[here, :], down_ref[:, head:]).astype(BF16)


def split(planes_in, head):
    keys = [x[i : i + TILE, :head] for x in planes_in for i in range(0, x.shape[0], TILE)]
    values = [x[i : i + TILE, head:] for x in planes_in for i in range(0, x.shape[0], TILE)]
    vt = jnp.concatenate([x[:, head:].T for x in planes_in], axis=1)
    return keys, values, vt


def forward(across, planes, state):
    head, wide = across.shape[0] // 2, across.shape[1]
    n = len(planes)
    rows = planes[0].shape[0]
    factor = head ** (-0.5) * math.log2(math.e)

    def body(*refs):
        qt_ref, gt_ref = refs[0].at[:head, :], refs[0].at[head:, :]
        old_ref, state_ref, score_ref, pgrad_ref = refs[1 + n :]
        keys, values, vt = split(refs[1 : 1 + n], head)
        highs = emit_scores(keys, qt_ref, score_ref, lambda s: s)
        for part, high in zip(parts_of(qt_ref), highs):
            merged = merge(old_ref, part, high, len(keys), vt, score_ref, factor)
            put_state(state_ref, part, *merged, old_ref[head + 2 : head + 3, part])
        emit_pgrads(values, gt_ref, pgrad_ref)

    kept = ((n * rows, wide), F32)
    state, *kept = call(body, [((head + 8, wide), F32), kept, kept], [], "forward", across, *planes, state)
    return state, kept


def turn(across, down, planes, state, tokens):
    head, wide = across.shape[0] // 2, across.shape[1]
    n = len(planes)
    rows = n * planes[0].shape[0]
    scale = head ** (-0.5)
    factor = scale * math.log2(math.e)

    def body(*refs):
        qt_ref, gt_ref, down_ref = refs[0].at[:head, :], refs[0].at[head:, :], refs[1]
        old_ref, back_ref, att_ref, terms_ref, dscore_ref, score_ref, prob_ref = refs[2 + n :]
        keys, values, vt = split(refs[2 : 2 + n], head)
        highs = emit_scores(keys, qt_ref, score_ref, lambda s: s)
        for part, high in zip(parts_of(qt_ref), highs):
            top, total, summed = merge(old_ref, part, high, len(keys), vt, score_ref, factor, keep=True)
            length = old_ref[head + 2 : head + 3, part]
            alive = token_of((1, WIDE), tokens) < length.astype(jnp.int32)
            share = 1.0 / total
            attended = jnp.where(alive, summed * share, 0.0).astype(BF16)
            inner = gt_ref[:, part].astype(F32) * attended.astype(F32)
            inner = jnp.sum(inner, axis=0, keepdims=True)
            back_ref[0:1, part] = top * factor + jnp.log2(total)
            back_ref[1:2, part] = inner
            back_ref[2:3, part] = length
            att_ref[:, part] = attended
            for i, v in enumerate(values):
                here = slice(i * TILE, (i + 1) * TILE)
                prob = score_ref[here, part] * share
                prob_ref[here, part] = prob.astype(BF16)
                dscore_ref[here, part] = (prob * (mm(v, gt_ref[:, part]) - inner)).astype(BF16)
        emit_terms(prob_ref, dscore_ref, down_ref, terms_ref, scale)

    return call(
        body,
        [((8, wide), F32), ((head, wide), BF16), ((rows, 2 * head), BF16), ((rows, wide), BF16)],
        [pltpu.VMEM((rows, wide), F32), pltpu.VMEM((rows, wide), BF16)],
        "turn",
        across, down, *planes, state,
    )


def backward(down, back, kept, n):
    wide, head = down.shape[0], down.shape[1] // 2
    rows = kept[0].shape[0] // n
    scale = head ** (-0.5)
    factor = scale * math.log2(math.e)

    def body(*refs):
        down_ref, back_ref, score_ref, pgrad_ref = refs[:4]
        terms, dscores, prob_ref = refs[4 : 4 + n], refs[4 + n : 4 + 2 * n], refs[-1]
        for j in range(n):
            here = slice(j * rows, (j + 1) * rows)
            prob, pgrads = prob_ref.at[here, :], pgrad_ref.at[here, :]
            emit_dscores(
                score_ref.at[here, :],
                lambda i, part: pgrads[i * TILE : (i + 1) * TILE, part],
                back_ref,
                prob,
                dscores[j],
                factor,
            )
            emit_terms(prob, dscores[j], down_ref, terms[j], scale)

    out = call(
        body,
        [((rows, 2 * head), BF16)] * n + [((rows, wide), BF16)] * n,
        [pltpu.VMEM((n * rows, wide), BF16)],
        "backward",
        down, back, *kept,
    )
    return out[:n], out[n:]


def finish(across, down, back, keys, values, attended, planes, dscores):
    head, wide = across.shape[0] // 2, across.shape[1]
    tokens = keys.shape[0]
    n = len(planes)
    scale = head ** (-0.5)
    factor = scale * math.log2(math.e)

    def body(*refs):
        across_ref, down_ref, back_ref, k_ref, v_ref, att_ref = refs[:6]
        planes_in, dscores_in = refs[6 : 6 + n], refs[6 + n : -6]
        qt_ref, gt_ref = across_ref.at[:head, :], across_ref.at[head:, :]
        out_ref, dq_ref, dk_ref, dv_ref, prob_ref, dscore_ref = refs[-6:]
        kt = k_ref[...].T
        kts, planes_kt = [x[:, :head].T for x in planes_in], []
        for d in dscores_in:
            group = [kts.pop(0)]
            while sum(k.shape[1] for k in group) < d.shape[0]:
                group.append(kts.pop(0))
            planes_kt.append(jnp.concatenate(group, axis=1))
        for part in parts_of(qt_ref):
            length = back_ref[2:3, part].astype(jnp.int32)
            scores = causal(mm(k_ref[...], qt_ref[:, part]), tokens, length)
            pgrad = mm(v_ref[...], gt_ref[:, part])
            prob, dscore = probabilities(scores, pgrad, back_ref, part, factor)
            prob_ref[:, part] = prob
            dscore_ref[:, part] = dscore
            total = mm(kt, dscore)
            for k, d in zip(planes_kt, dscores_in):
                total = total + mm(k, d[:, part])
            out = (total * scale).astype(BF16)
            for i in range(WIDE // tokens):
                h = part.start // tokens + i
                dq_ref[:, h * head : (h + 1) * head] = out[:, i * tokens : (i + 1) * tokens].T
                out_ref[:, h * head : (h + 1) * head] = att_ref[:, h * tokens : (h + 1) * tokens].T
        dk_ref[...] = (mm(dscore_ref[...], down_ref[:, :head]) * scale).astype(BF16)
        dv_ref[...] = mm(prob_ref[...], down_ref[:, head:]).astype(BF16)

    flat = ((tokens, wide // tokens * head), BF16)
    return call(
        body,
        [flat, flat, (keys.shape, BF16), (values.shape, BF16)],
        [pltpu.VMEM((tokens, wide), BF16), pltpu.VMEM((tokens, wide), BF16)],
        "finish",
        across, down, back, keys, values, attended, *planes, *dscores,
    )


def spread(keys, values, count):
    rows, head = keys.shape

    def body(k_ref, v_ref, out_ref):
        for i in range(count):
            out_ref[i, :, :head] = k_ref[...]
            out_ref[i, :, head:] = v_ref[...]

    return call(body, [((count, rows, 2 * head), BF16)], [], "spread", keys, values, limit=ALL_VMEM_BYTES)[0]


def collect(parts, head):
    def body(in_ref, key_ref, value_ref):
        total = jnp.sum(in_ref[...].astype(F32), axis=0).astype(BF16)
        key_ref[...] = total[:, :head]
        value_ref[...] = total[:, head:]

    shape = ((parts.shape[1], head), BF16)
    return call(body, [shape, shape], [], "collect", parts)


Z_SIZE = 8


def shards(queries, resp_keys, resp_values, prefix_keys, prefix_values, out_grad, lengths, loss_mask):
    group_count = lax.axis_size("grp")
    z_size = Z_SIZE
    y_size = group_count // z_size
    z_groups = [[y * z_size + z for z in range(z_size)] for y in range(y_size)]

    def along_y(x, partner):
        pairs = [(y * z_size + z, partner(y) % y_size * z_size + z) for y in range(y_size) for z in range(z_size)]
        return lax.ppermute(x, "grp", pairs)

    def one_way(y):
        return y + 1 if y % 2 == 0 else y - 1

    def other_way(y):
        return y - 1 if y % 2 == 0 else y + 1

    def across_ring(y):
        return y + 2

    def along_z(x):
        return lax.all_to_all(x, "grp", 0, 0, axis_index_groups=z_groups, tiled=True)

    own_keys, own_values = resp_keys[0], resp_values[0]
    tokens = own_keys.shape[0]
    rows, head = prefix_keys.shape
    mine = along_z(spread(prefix_keys, prefix_values, z_size)).reshape(z_size * rows, 2 * head)
    across, down, state = start(lengths, queries[0], out_grad[0], loss_mask, own_keys, own_values)
    mine, state = lax.optimization_barrier((mine, state))
    near, other = along_y(mine, one_way), along_y(mine, other_way)
    state, mine_kept = forward(across, [mine], state)
    half = mine.shape[0] // 2
    near, state = lax.optimization_barrier((near, state))
    far = [along_y(near[:half], other_way)]
    other, state = lax.optimization_barrier((other, state))
    far.append(along_y(other[half:], one_way))
    state, kept = forward(across, [near, other], state)
    back, attended, far_terms, far_ds = turn(across, down, far, state, tokens)
    far_terms = along_y(far_terms, across_ring)
    (near_terms, other_terms), (near_ds, other_ds) = backward(down, back, kept, 2)
    near_terms, other_terms = along_y(near_terms, one_way), along_y(other_terms, other_way)
    (mine_terms,), (mine_ds,) = backward(down, back, mine_kept, 1)
    attended, query_grad, key_grad, value_grad = finish(
        across, down, back, own_keys, own_values, attended,
        [mine, near, other, *far], [mine_ds, near_ds, other_ds, far_ds],
    )
    mine_terms, attended, query_grad, key_grad, value_grad = lax.optimization_barrier(
        (mine_terms, attended, query_grad, key_grad, value_grad)
    )
    part = sum(x.astype(F32) for x in (mine_terms, near_terms, other_terms, far_terms)).astype(BF16)
    key_share, value_share = collect(along_z(part.reshape(z_size, rows, 2 * head)), head)
    return (attended[None], query_grad[None], key_grad[None], value_grad[None], key_share, value_share)


def solution(mesh):
    placed = (
        P(("prompt", "grp"), None, None),
        P(("prompt", "grp"), None, None),
        P(("prompt", "grp"), None, None),
        P(("prompt", "grp"), None),
        P(("prompt", "grp"), None),
        P(("prompt", "grp"), None, None),
        P("prompt"),
        P(("prompt", "grp"), None),
    )
    return jax.shard_map(
        shards,
        mesh=mesh,
        in_specs=placed,
        out_specs=(
            P(("prompt", "grp"), None, None),
            P(("prompt", "grp"), None, None),
            P(("prompt", "grp"), None, None),
            P(("prompt", "grp"), None, None),
            P(("prompt", "grp"), None),
            P(("prompt", "grp"), None),
        ),
        check_vma=False,
    )
```

```python
import math
import jax, jax.numpy as jnp
from jax import lax
from jax.experimental import pallas as pl
from jax.experimental.pallas import tpu as pltpu
from jax.sharding import PartitionSpec as P

F32 = jnp.float32
BF16 = jnp.bfloat16
NEG_BIG = -1e30
TILE = 256
WIDE = 512
VMEM_BYTES = 14 * 2**20
ALL_VMEM_BYTES = 57 * 2**20


def mm(left, right):
    return jnp.dot(left, right, preferred_element_type=F32)


def fold(tile):
    return tile.reshape(tile.shape[0] // 8, 8, tile.shape[1])


def token_of(shape, tokens):
    return lax.rem(lax.broadcasted_iota(jnp.int32, shape, 1), tokens)


def causal(scores, tokens, length):
    key = lax.broadcasted_iota(jnp.int32, scores.shape, 0)
    return jnp.where((key <= token_of(scores.shape, tokens)) & (key < length), scores, NEG_BIG)


def own_length(lengths_ref):
    return lengths_ref[lax.axis_index("grp")]


def parts_of(ref):
    return [slice(i, i + WIDE) for i in range(0, ref.shape[1], WIDE)]


def call(body, out_shape, scratch, name, *args, space=pltpu.VMEM, limit=VMEM_BYTES):
    specs = [pl.BlockSpec(memory_space=pltpu.SMEM if a.ndim == 1 else space) for a in args]
    return pl.pallas_call(
        body,
        in_specs=specs,
        out_specs=[pl.BlockSpec(memory_space=pltpu.VMEM)] * len(out_shape),
        out_shape=[jax.ShapeDtypeStruct(s, d) for s, d in out_shape],
        scratch_shapes=scratch,
        compiler_params=pltpu.CompilerParams(vmem_limit_bytes=limit),
        name=name,
    )(*args)


def put_state(state_ref, part, top, total, summed, length):
    head = state_ref.shape[0] - 8
    state_ref[:head, part] = summed
    state_ref[head : head + 1, part] = top
    state_ref[head + 1 : head + 2, part] = total
    state_ref[head + 2 : head + 3, part] = length


def emit_scores(keys, qt_ref, score_ref, mask):
    highs = []
    for part in parts_of(qt_ref):
        high = None
        for i, k in enumerate(keys):
            scores = mask(mm(k, qt_ref[:, part]))
            score_ref[i * TILE : (i + 1) * TILE, part] = scores
            peak = jnp.max(fold(scores), axis=0)
            high = peak if high is None else jnp.maximum(high, peak)
        highs.append(high)
    return highs


def emit_sums(n, top, vt, score_ref, part, factor, keep=False):
    total, summed = None, None
    for i in range(n):
        weights = jnp.exp2((score_ref[i * TILE : (i + 1) * TILE, part] - top) * factor)
        if keep:
            score_ref[i * TILE : (i + 1) * TILE, part] = weights
        here = jnp.sum(fold(weights), axis=0)
        total = here if total is None else total + here
        here = mm(vt[:, i * TILE : (i + 1) * TILE], weights.astype(BF16))
        summed = here if summed is None else summed + here
    return jnp.sum(total, axis=0, keepdims=True), summed


def start(lengths, queries, grads, mask, keys, values):
    tokens, width = queries.shape
    head = keys.shape[1]
    heads = width // head
    wide = heads * tokens
    factor = head ** (-0.5) * math.log2(math.e)

    def body(
        lengths_ref, q_in, g_in, mask_in, k_in, v_in,
        across_ref, down_ref, state_ref,
        q_ref, g_ref, mask_ref, k_ref, v_ref, score_ref, sems,
    ):
        copies = [
            pltpu.make_async_copy(a, b, sems.at[i])
            for i, (a, b) in enumerate(
                [(q_in, q_ref), (k_in, k_ref), (v_in, v_ref), (mask_in, mask_ref), (g_in, g_ref)]
            )
        ]
        for c in copies:
            c.start()
        length = own_length(lengths_ref)
        qt_ref, gt_ref = across_ref.at[:head, :], across_ref.at[head:, :]
        copies[0].wait()
        for h in range(heads):
            cols, rows = slice(h * head, (h + 1) * head), slice(h * tokens, (h + 1) * tokens)
            q = q_ref[:, cols]
            down_ref[rows, :head] = q
            qt_ref[:, rows] = q.T
        copies[1].wait()
        copies[2].wait()
        highs = emit_scores([k_ref[...]], qt_ref, score_ref, lambda s: causal(s, tokens, length))
        vt = v_ref[...].T
        for part, high in zip(parts_of(qt_ref), highs):
            top = jnp.max(high, axis=0, keepdims=True)
            total, summed = emit_sums(1, top, vt, score_ref, part, factor)
            put_state(state_ref, part, top, total, summed, jnp.full((1, WIDE), length.astype(F32)))
        copies[3].wait()
        copies[4].wait()
        kept = (token_of((1, tokens), tokens) < length) & (mask_ref[...] == 1)
        for h in range(heads):
            cols, rows = slice(h * head, (h + 1) * head), slice(h * tokens, (h + 1) * tokens)
            gt = jnp.where(kept, g_ref[:, cols].T, jnp.zeros((), BF16))
            gt_ref[:, rows] = gt
            down_ref[rows, head:] = gt.T

    args = [queries, grads, mask, keys, values]
    return call(
        body,
        [((2 * head, wide), BF16), ((wide, 2 * head), BF16), ((head + 8, wide), F32)],
        [pltpu.VMEM(x.shape, x.dtype) for x in args]
        + [pltpu.VMEM((tokens, wide), F32), pltpu.SemaphoreType.DMA((5,))],
        "start",
        lengths,
        *args,
        space=pltpu.HBM,
        limit=ALL_VMEM_BYTES,
    )


def emit_pgrads(values, gt_ref, pgrad_ref):
    for part in parts_of(gt_ref):
        for i, v in enumerate(values):
            pgrad_ref[i * TILE : (i + 1) * TILE, part] = mm(v, gt_ref[:, part])


def merge(state_ref, part, high, n, vt, score_ref, factor, keep=False):
    head = state_ref.shape[0] - 8
    before = state_ref[head : head + 1, part]
    top = jnp.maximum(jnp.max(high, axis=0, keepdims=True), before)
    total, summed = emit_sums(n, top, vt, score_ref, part, factor, keep)
    shrink = jnp.exp2((before - top) * factor)
    return top, total + shrink * state_ref[head + 1 : head + 2, part], summed + shrink * state_ref[:head, part]


def probabilities(scores, pgrad, back_ref, part, factor):
    prob = jnp.exp2(scores * factor - back_ref[0:1, part])
    return prob.astype(BF16), (prob * (pgrad - back_ref[1:2, part])).astype(BF16)


def emit_dscores(score_ref, pgrad, back_ref, prob_ref, dscore_ref, factor):
    for part in parts_of(score_ref):
        for i in range(score_ref.shape[0] // TILE):
            here = slice(i * TILE, (i + 1) * TILE)
            prob, dscore = probabilities(score_ref[here, part], pgrad(i, part), back_ref, part, factor)
            prob_ref[here, part] = prob
            dscore_ref[here, part] = dscore


def emit_terms(prob_ref, dscore_ref, down_ref, terms_ref, scale):
    head = down_ref.shape[1] // 2
    for i in range(0, prob_ref.shape[0], TILE):
        here = slice(i, i + TILE)
        terms_ref[here, :head] = (mm(dscore_ref[here, :], down_ref[:, :head]) * scale).astype(BF16)
        terms_ref[here, head:] = mm(prob_ref[here, :], down_ref[:, head:]).astype(BF16)


def split(planes_in, head):
    keys = [x[i : i + TILE, :head] for x in planes_in for i in range(0, x.shape[0], TILE)]
    values = [x[i : i + TILE, head:] for x in planes_in for i in range(0, x.shape[0], TILE)]
    vt = jnp.concatenate([x[:, head:].T for x in planes_in], axis=1)
    return keys, values, vt


def forward(across, planes, state):
    head, wide = across.shape[0] // 2, across.shape[1]
    n = len(planes)
    rows = planes[0].shape[0]
    factor = head ** (-0.5) * math.log2(math.e)

    def body(*refs):
        qt_ref, gt_ref = refs[0].at[:head, :], refs[0].at[head:, :]
        old_ref, state_ref, score_ref, pgrad_ref = refs[1 + n :]
        keys, values, vt = split(refs[1 : 1 + n], head)
        highs = emit_scores(keys, qt_ref, score_ref, lambda s: s)
        for part, high in zip(parts_of(qt_ref), highs):
            merged = merge(old_ref, part, high, len(keys), vt, score_ref, factor)
            put_state(state_ref, part, *merged, old_ref[head + 2 : head + 3, part])
        emit_pgrads(values, gt_ref, pgrad_ref)

    kept = ((n * rows, wide), F32)
    state, *kept = call(body, [((head + 8, wide), F32), kept, kept], [], "forward", across, *planes, state)
    return state, kept


def turn(across, down, planes, state, tokens):
    head, wide = across.shape[0] // 2, across.shape[1]
    n = len(planes)
    rows = n * planes[0].shape[0]
    scale = head ** (-0.5)
    factor = scale * math.log2(math.e)

    def body(*refs):
        qt_ref, gt_ref, down_ref = refs[0].at[:head, :], refs[0].at[head:, :], refs[1]
        old_ref, back_ref, att_ref, terms_ref, dscore_ref, score_ref, prob_ref = refs[2 + n :]
        keys, values, vt = split(refs[2 : 2 + n], head)
        highs = emit_scores(keys, qt_ref, score_ref, lambda s: s)
        for part, high in zip(parts_of(qt_ref), highs):
            top, total, summed = merge(old_ref, part, high, len(keys), vt, score_ref, factor, keep=True)
            length = old_ref[head + 2 : head + 3, part]
            alive = token_of((1, WIDE), tokens) < length.astype(jnp.int32)
            share = 1.0 / total
            attended = jnp.where(alive, summed * share, 0.0).astype(BF16)
            inner = gt_ref[:, part].astype(F32) * attended.astype(F32)
            inner = jnp.sum(inner, axis=0, keepdims=True)
            back_ref[0:1, part] = top * factor + jnp.log2(total)
            back_ref[1:2, part] = inner
            back_ref[2:3, part] = length
            att_ref[:, part] = attended
            for i, v in enumerate(values):
                here = slice(i * TILE, (i + 1) * TILE)
                prob = score_ref[here, part] * share
                prob_ref[here, part] = prob.astype(BF16)
                dscore_ref[here, part] = (prob * (mm(v, gt_ref[:, part]) - inner)).astype(BF16)
        emit_terms(prob_ref, dscore_ref, down_ref, terms_ref, scale)

    return call(
        body,
        [((8, wide), F32), ((head, wide), BF16), ((rows, 2 * head), BF16), ((rows, wide), BF16)],
        [pltpu.VMEM((rows, wide), F32), pltpu.VMEM((rows, wide), BF16)],
        "turn",
        across, down, *planes, state,
    )


def backward(down, back, kept, n):
    wide, head = down.shape[0], down.shape[1] // 2
    rows = kept[0].shape[0] // n
    scale = head ** (-0.5)
    factor = scale * math.log2(math.e)

    def body(*refs):
        down_ref, back_ref, score_ref, pgrad_ref = refs[:4]
        terms, dscores, prob_ref = refs[4 : 4 + n], refs[4 + n : 4 + 2 * n], refs[-1]
        for j in range(n):
            here = slice(j * rows, (j + 1) * rows)
            prob, pgrads = prob_ref.at[here, :], pgrad_ref.at[here, :]
            emit_dscores(
                score_ref.at[here, :],
                lambda i, part: pgrads[i * TILE : (i + 1) * TILE, part],
                back_ref,
                prob,
                dscores[j],
                factor,
            )
            emit_terms(prob, dscores[j], down_ref, terms[j], scale)

    out = call(
        body,
        [((rows, 2 * head), BF16)] * n + [((rows, wide), BF16)] * n,
        [pltpu.VMEM((n * rows, wide), BF16)],
        "backward",
        down, back, *kept,
    )
    return out[:n], out[n:]


def finish(across, down, back, keys, values, attended, kept, planes, dscores):
    head, wide = across.shape[0] // 2, across.shape[1]
    tokens = keys.shape[0]
    n = len(planes)
    scale = head ** (-0.5)
    factor = scale * math.log2(math.e)

    def body(*refs):
        across_ref, down_ref, back_ref, k_ref, v_ref, att_ref, first_score_ref, first_pgrad_ref = refs[:8]
        first_prob_ref, first_dscore_ref = refs[-2:]
        refs = refs[:-2]
        planes_in, dscores_in = refs[8 : 8 + n], [first_dscore_ref, *refs[8 + n : -7]]
        terms_ref, refs = refs[-7], refs[:-7] + refs[-6:]
        emit_dscores(
            first_score_ref,
            lambda i, part: first_pgrad_ref[i * TILE : (i + 1) * TILE, part],
            back_ref,
            first_prob_ref,
            first_dscore_ref,
            factor,
        )
        emit_terms(first_prob_ref, first_dscore_ref, down_ref, terms_ref, scale)
        qt_ref, gt_ref = across_ref.at[:head, :], across_ref.at[head:, :]
        out_ref, dq_ref, dk_ref, dv_ref, prob_ref, dscore_ref = refs[-6:]
        kt = k_ref[...].T
        kts, planes_kt = [x[:, :head].T for x in planes_in], []
        for d in dscores_in:
            group = [kts.pop(0)]
            while sum(k.shape[1] for k in group) < d.shape[0]:
                group.append(kts.pop(0))
            planes_kt.append(jnp.concatenate(group, axis=1))
        for part in parts_of(qt_ref):
            length = back_ref[2:3, part].astype(jnp.int32)
            scores = causal(mm(k_ref[...], qt_ref[:, part]), tokens, length)
            pgrad = mm(v_ref[...], gt_ref[:, part])
            prob, dscore = probabilities(scores, pgrad, back_ref, part, factor)
            prob_ref[:, part] = prob
            dscore_ref[:, part] = dscore
            total = mm(kt, dscore)
            for k, d in zip(planes_kt, dscores_in):
                total = total + mm(k, d[:, part])
            out = (total * scale).astype(BF16)
            for i in range(WIDE // tokens):
                h = part.start // tokens + i
                dq_ref[:, h * head : (h + 1) * head] = out[:, i * tokens : (i + 1) * tokens].T
                out_ref[:, h * head : (h + 1) * head] = att_ref[:, h * tokens : (h + 1) * tokens].T
        dk_ref[...] = (mm(dscore_ref[...], down_ref[:, :head]) * scale).astype(BF16)
        dv_ref[...] = mm(prob_ref[...], down_ref[:, head:]).astype(BF16)

    flat = ((tokens, wide // tokens * head), BF16)
    return call(
        body,
        [(planes[0].shape, BF16), flat, flat, (keys.shape, BF16), (values.shape, BF16)],
        [pltpu.VMEM((tokens, wide), BF16)] * 2 + [pltpu.VMEM((planes[0].shape[0], wide), BF16)] * 2,
        "finish",
        across, down, back, keys, values, attended, *kept, *planes, *dscores,
    )


def spread(keys, values, count):
    rows, head = keys.shape

    def body(k_ref, v_ref, out_ref):
        for i in range(count):
            out_ref[i, :, :head] = k_ref[...]
            out_ref[i, :, head:] = v_ref[...]

    return call(body, [((count, rows, 2 * head), BF16)], [], "spread", keys, values, limit=ALL_VMEM_BYTES)[0]


def collect(parts, head):
    def body(in_ref, key_ref, value_ref):
        total = jnp.sum(in_ref[...].astype(F32), axis=0).astype(BF16)
        key_ref[...] = total[:, :head]
        value_ref[...] = total[:, head:]

    shape = ((parts.shape[1], head), BF16)
    return call(body, [shape, shape], [], "collect", parts)


Z_SIZE = 8


def shards(queries, resp_keys, resp_values, prefix_keys, prefix_values, out_grad, lengths, loss_mask):
    group_count = lax.axis_size("grp")
    z_size = Z_SIZE
    y_size = group_count // z_size
    z_groups = [[y * z_size + z for z in range(z_size)] for y in range(y_size)]

    def along_y(x, partner):
        pairs = [(y * z_size + z, partner(y) % y_size * z_size + z) for y in range(y_size) for z in range(z_size)]
        return lax.ppermute(x, "grp", pairs)

    def one_way(y):
        return y + 1 if y % 2 == 0 else y - 1

    def other_way(y):
        return y - 1 if y % 2 == 0 else y + 1

    def across_ring(y):
        return y + 2

    def along_z(x):
        return lax.all_to_all(x, "grp", 0, 0, axis_index_groups=z_groups, tiled=True)

    own_keys, own_values = resp_keys[0], resp_values[0]
    tokens = own_keys.shape[0]
    rows, head = prefix_keys.shape
    mine = along_z(spread(prefix_keys, prefix_values, z_size)).reshape(z_size * rows, 2 * head)
    across, down, state = start(lengths, queries[0], out_grad[0], loss_mask, own_keys, own_values)
    mine, state = lax.optimization_barrier((mine, state))
    near, other = along_y(mine, one_way), along_y(mine, other_way)
    state, mine_kept = forward(across, [mine], state)
    half = mine.shape[0] // 2
    near, state = lax.optimization_barrier((near, state))
    far = [along_y(near[:half], other_way)]
    other, state = lax.optimization_barrier((other, state))
    far.append(along_y(other[half:], one_way))
    state, kept = forward(across, [near, other], state)
    back, attended, far_terms, far_ds = turn(across, down, far, state, tokens)
    far_terms = along_y(far_terms, across_ring)
    (near_terms, other_terms), (near_ds, other_ds) = backward(down, back, kept, 2)
    near_terms, other_terms = along_y(near_terms, one_way), along_y(other_terms, other_way)
    mine_terms, attended, query_grad, key_grad, value_grad = finish(
        across, down, back, own_keys, own_values, attended, mine_kept,
        [mine, near, other, *far], [near_ds, other_ds, far_ds],
    )
    mine_terms, attended, query_grad, key_grad, value_grad = lax.optimization_barrier(
        (mine_terms, attended, query_grad, key_grad, value_grad)
    )
    part = sum(x.astype(F32) for x in (mine_terms, near_terms, other_terms, far_terms)).astype(BF16)
    key_share, value_share = collect(along_z(part.reshape(z_size, rows, 2 * head)), head)
    return (attended[None], query_grad[None], key_grad[None], value_grad[None], key_share, value_share)


def solution(mesh):
    placed = (
        P(("prompt", "grp"), None, None),
        P(("prompt", "grp"), None, None),
        P(("prompt", "grp"), None, None),
        P(("prompt", "grp"), None),
        P(("prompt", "grp"), None),
        P(("prompt", "grp"), None, None),
        P("prompt"),
        P(("prompt", "grp"), None),
    )
    return jax.shard_map(
        shards,
        mesh=mesh,
        in_specs=placed,
        out_specs=(
            P(("prompt", "grp"), None, None),
            P(("prompt", "grp"), None, None),
            P(("prompt", "grp"), None, None),
            P(("prompt", "grp"), None, None),
            P(("prompt", "grp"), None),
            P(("prompt", "grp"), None),
        ),
        check_vma=False,
    )
```
